32 devices in a mesh: groups: 2 (over y), ep: 8 (over z, x), tp: 2 (over core).
Axes of the slice: x: 2, y: 2, z: 4, core: 2. Of those that a mesh axis runs over, the one named last changes fastest.
Arguments:
- tokens: bfloat16 [2048, 1536], P(('groups', 'ep', 'tp')), parts along dimension 0, may hold values from -16 to 16
- expert_ids: int32 [2048, 4], P(('groups', 'ep', 'tp')), parts along dimension 0, may hold values from 0 to 7, all different within a row; in each aligned block of 64 rows (0 to 63, 64 to 127, ...) at most 64 rows name the same one
- combine_weights: float32 [2048, 4], P(('groups', 'ep', 'tp')), parts along dimension 0, may hold values from 0.1 to 1
- gate_weight: bfloat16 [8, 1536, 1536], P(None, 'ep', 'tp'), may hold values from -0.15625 to 0.15625
- up_weight: bfloat16 [8, 1536, 1536], P(None, 'ep', 'tp'), may hold values from -0.15625 to 0.15625
Outputs:
- expert_mix: bfloat16 [2048, 1536], P(('groups', 'ep', 'tp')), parts along dimension 0
The draws below stay inside these ranges and needn't reach their ends.
There are 2 independent parts, one for each index of `groups`. The reference program is written for one: setup_inputs(seed, part) draws one part's arguments, and reference() takes and returns one part's arrays. A program takes and returns all parts, laid end to end along the dimension named above; an argument that names none is the same for every part. Nothing has to cross between parts.
Inputs may be any that keep to these rules, and one draw needn't show every extreme that they name: `expert_ids`: each row names 4 different experts. In the rows of one device no expert is named more than 64 times, and in some device's rows some expert is named exactly 64 times.
All inputs are finite; a program needn't handle non-finite values.
Results may differ from the reference program's by a relative error of at most 0.008.
Values may be sent and summed in bfloat16 or wider, within the bound.
No kernel may reach another device: no remote copies, remote signals or barrier semaphores. Data moves between devices by JAX's collectives and lax.ppermute only.
A program may use at most 256 MiB of HBM per device.

```python
import math
import jax
import jax.numpy as jnp
import numpy as np
from jax import lax

D = 1536
FF = 1536
TOP = 4
TOK_DEV = 64
EXPERTS = 8
SLOTS = 64
TOKENS = 1024


def draw_tokens(key, part):
    key = jax.random.fold_in(key, 11)
    scale_key = jax.random.fold_in(key, 1)
    value_key = jax.random.fold_in(key, 2)
    row_scale = jnp.exp(jax.random.uniform(scale_key, (TOKENS, 1), jnp.float32, jnp.log(0.5), jnp.log(4.0)))
    values = jax.random.normal(value_key, (TOKENS, D), jnp.float32)
    return jnp.clip(values * row_scale, -16.0, 16.0).astype(jnp.bfloat16)


def shard_levels(own_key, shape, cuts, least, high):
    def one(position, shards_of):
        steps = jax.random.uniform(jax.random.fold_in(jax.random.fold_in(own_key, 6), position), (shards_of,), jnp.float32, least / len(cuts), high / len(cuts))
        return jnp.repeat(jnp.exp(steps), shape[position] // shards_of).reshape((-1,) + (1,) * (len(shape) - position - 1))

    gain = one(*cuts[0])
    for cut in cuts[1:]:
        gain = gain * one(*cut)
    return gain


def assign_block(key, own, number, rows, number_of, top, reach, slope):
    sequence = jax.random.permutation(key, number_of)
    heavy_load, usual = shares(number_of, rows * top, reach, slope, True), shares(number_of, rows * top, reach, slope, False)
    places = jnp.arange(number_of)

    def named(tallies, turn):
        used = int((tallies > 0).sum())
        fixed = max(1, used // 4)
        passed = fixed + (places - fixed + turn * (used - fixed)) % max(1, number_of - fixed)
        return jnp.zeros((number_of,), jnp.int32).at[sequence[jnp.where(places < fixed, places, passed)]].set(jnp.asarray(tallies, jnp.int32))

    tallies = jnp.where(number % 4 == 0, named(heavy_load, number // 4), named(usual, number - number // 4 - 1))
    mixed = jax.random.permutation(jax.random.fold_in(own, 3), number_of)
    source_of, sink = mixed[0:number_of // 2 * 2:2], mixed[1:number_of // 2 * 2:2]
    margin = jnp.minimum(tallies[source_of] - 1, reach - tallies[sink]) // 2
    margin = jnp.where((source_of == sequence[0]) | (sink == sequence[0]) | (tallies[sink] == 0), 0, jnp.maximum(margin, 0))
    passed = jax.random.randint(jax.random.fold_in(own, 4), (number_of // 2,), 0, 1 << 20) % (margin + 1)
    tallies = tallies.at[source_of].add(-passed).at[sink].add(passed)
    members = jnp.searchsorted(jnp.cumsum(tallies), jnp.arange(rows * top), side="right").astype(jnp.int32)
    listing = members.reshape(top, rows).T
    listing = listing[jax.random.permutation(jax.random.fold_in(own, 1), rows)]
    turn = jax.random.randint(jax.random.fold_in(own, 2), (rows, 1), 0, top)
    return jnp.take_along_axis(listing, (jnp.arange(top)[None, :] + turn) % top, axis=1)


def shares(amount, total, bound, lean, full):
    weights = [(1 << 20) // math.isqrt(grade ** lean) + 1 for grade in range(1, amount + 1)]
    largest = bound if full else min(bound, max(-(-total // amount), total * weights[0] // sum(weights)))
    least = 1 if total - largest >= amount - 1 else 0
    holding, rest = [largest] + [least] * (amount - 1), total - largest - least * (amount - 1)
    while rest > 0:
        movable = [i for i in range(1, amount) if holding[i] < largest] or [i for i in range(1, amount) if holding[i] < bound]
        pool, left = sum([weights[i] for i in movable]), rest
        for i in movable:
            extra = min(bound - holding[i], max(1, left * weights[i] // pool), rest)
            holding[i] = holding[i] + extra
            rest = rest - extra
    return np.array(holding)


def scatter_about(key, dims, scale, reach, split=(), kind=jnp.bfloat16):
    level = shard_levels(key, dims, split, -0.22, 0.18) if split else 1.0
    array = jax.random.normal(key, dims, jnp.float32) * scale * level
    return jnp.minimum(jnp.maximum(array, -reach), reach).astype(kind)


def setup_inputs(seed: int = 0, part: int = 0) -> dict:
    splits = jax.random.split(jax.random.key(seed), 6)
    part_splits = jax.random.split(jax.random.fold_in(splits[5], part), 6)
    tokens = draw_tokens(jax.random.fold_in(jax.random.fold_in(splits[5], part), 71), part)
    expert_ids_keys = jax.random.split(jax.random.fold_in(part_splits[1], 1), TOKENS // TOK_DEV)
    expert_ids_turns = jax.random.permutation(jax.random.fold_in(part_splits[1], 3), TOKENS // TOK_DEV)
    expert_ids = jax.vmap(lambda own, number: assign_block(jax.random.fold_in(part_splits[1], 2), own, number, TOK_DEV, EXPERTS, TOP, SLOTS, 2))(expert_ids_keys, expert_ids_turns).reshape((TOKENS, TOP))
    combine_weights = jnp.clip(jnp.exp(math.log(1.0) - 2.3025851 * jax.random.uniform(part_splits[2], (TOKENS, TOP), jnp.float32) ** shard_levels(part_splits[2], (TOKENS, TOP), ((0, 16),), -0.2, 0.2)), 0.1, 1.0)
    gate_weight = scatter_about(splits[3], (EXPERTS, FF, D), D ** -0.5, 0.15625, ((1, 8), (2, 2)))
    up_weight = scatter_about(splits[4], (EXPERTS, FF, D), D ** -0.5, 0.15625, ((1, 8), (2, 2)))
    return {"tokens": tokens, "expert_ids": expert_ids, "combine_weights": combine_weights, "gate_weight": gate_weight, "up_weight": up_weight}


THRESHOLDS = (0.25, 0.75, 1.25, 1.75, 2.5, 3.5, 5.0)
STEPS_UP = (0.5, 0.5, 0.5, 0.5, 1.0, 1.0, 2.0)
LIMIT = 7.0


def block_scale(largest):
    scale = jnp.full(largest.shape, 2.0 ** -40, jnp.float32)
    for exponent_value in range(-39, 9):
        power = 2.0 ** exponent_value
        scale = jnp.where(largest >= power, jnp.float32(power), scale)
    return scale * 0.25


def code_blocks(weight):
    shaped = weight.reshape(weight.shape[:-1] + (weight.shape[-1] // 32, 32))
    magnitude = jnp.abs(shaped).astype(jnp.float32)
    scale = block_scale(jnp.max(magnitude, axis=-1))[..., None]
    total = jnp.zeros(magnitude.shape, jnp.float32)
    for bound_value, step_value in zip(THRESHOLDS, STEPS_UP):
        total = total + jnp.where(magnitude > bound_value * scale, step_value, 0.0)
    signed = jnp.where(shaped < 0, -total, total) * scale
    return signed.reshape(weight.shape).astype(jnp.bfloat16)


def activate(gate_value, up_value):
    gate_clamped = jnp.minimum(gate_value, LIMIT)
    up_clamped = jnp.clip(up_value, -LIMIT, LIMIT)
    return gate_clamped * jax.nn.sigmoid(1.702 * gate_clamped) * (up_clamped + 1.0)


def reference(tokens, expert_ids, combine_weights, gate_weight, up_weight):
    blocks = TOKENS // TOK_DEV
    pair_count = TOK_DEV * TOP
    capacity = blocks * SLOTS
    chosen = expert_ids.reshape(blocks, pair_count)
    onehot = (chosen[:, :, None] == jnp.arange(EXPERTS, dtype=jnp.int32)).astype(jnp.int32)
    before = jnp.cumsum(onehot, axis=1, dtype=jnp.int32) - onehot
    ranking = jnp.sum(before * onehot, axis=2, dtype=jnp.int32)
    holder = jnp.arange(blocks, dtype=jnp.int32)[:, None]
    flat_slot = (chosen * capacity + holder * SLOTS + ranking).reshape(-1)
    token_of_pair = jnp.arange(blocks * pair_count, dtype=jnp.int32) // TOP
    owner_rows = jnp.full((EXPERTS * capacity,), TOKENS, jnp.int32).at[flat_slot].set(token_of_pair)
    owner_rows = owner_rows.reshape(EXPERTS, capacity)
    padded = jnp.concatenate([tokens, jnp.zeros((1, D), tokens.dtype)], axis=0)

    def expert_step(carry_value, inputs):
        slot_rows, gate_each, up_each = inputs
        features = padded[slot_rows]
        gate_coded = code_blocks(gate_each)
        up_coded = code_blocks(up_each)
        gate_value = jnp.dot(features, gate_coded.T, preferred_element_type=jnp.float32)
        up_value = jnp.dot(features, up_coded.T, preferred_element_type=jnp.float32)
        return carry_value, activate(gate_value, up_value).astype(jnp.bfloat16)

    _, actives = lax.scan(expert_step, jnp.zeros((), jnp.float32), (owner_rows, gate_weight, up_weight))
    values = actives.reshape(EXPERTS * capacity, FF)[flat_slot].reshape(TOKENS, TOP, FF)
    mixed = jnp.sum(values.astype(jnp.float32) * combine_weights.astype(jnp.float32)[:, :, None], axis=1)
    return mixed.astype(jnp.bfloat16)
```

```python
import functools

import jax
import jax.numpy as jnp
from jax import lax
from jax.experimental import pallas as pl
from jax.experimental.pallas import tpu as pltpu
from jax.sharding import PartitionSpec as P

THRESHOLDS = (0.25, 0.75, 1.25, 1.75, 2.5, 3.5, 5.0)
STEPS_UP = (0.5, 0.5, 0.5, 0.5, 1.0, 1.0, 2.0)
LIMIT = 7.0
LANES = 128
BLOCK = 32


def ring_place(owner, owners):
    return jnp.where(owner % 2 == 0, owner // 2, owners - 1 - owner // 2)


def ring_owner(place, owners):
    return jnp.where(place < owners // 2, 2 * place, 2 * (owners - 1 - place) + 1)


def ring_shift(owners, steps):
    order = list(range(0, owners, 2)) + list(range(1, owners, 2))[::-1]
    return [(order[p], order[(p + steps) % owners]) for p in range(owners)]


def ring_send(value, owners, steps):
    return lax.ppermute(value, "ep", ring_shift(owners, steps))


def code_columns(entries):
    depth, count = entries.shape
    blocks = entries.reshape(depth // BLOCK, BLOCK, count)
    largest = jnp.max(jnp.abs(blocks), axis=1, keepdims=True)
    largest = jnp.maximum(largest, 2.0**-40)
    lifted = largest * 2.0**23
    power = jnp.minimum((largest * 0.7 + lifted) - lifted, 2.0**8)
    lowered = blocks * (1.0 - 2.0**-12)
    top = power * 1.5
    lowered = jnp.minimum(jnp.maximum(lowered, -top), top)
    least = power * (0.25 * (1.0 + 2.0**-10))
    anchor = jnp.maximum(jnp.abs(lowered), least) * 2.0**22
    return ((lowered + anchor) - anchor).reshape(depth, count)


def code_kernel(gate_ref, up_ref, out_ref):
    depth = gate_ref.shape[2]
    for low in range(0, depth, 256):
        rows = [ref[expert, :, low : low + 256] for ref in (gate_ref, up_ref) for expert in range(ref.shape[0])]
        turned = jnp.concatenate(rows, axis=0).T.astype(jnp.float32)
        out_ref[low : low + 256, :] = code_columns(turned).astype(jnp.bfloat16)


def code_weights(gate, up, first_expert, count, tail):
    depth = gate.shape[2]
    if tail:
        block, tiles, index = (2, LANES // 2, depth), count // 2, lambda i: (first_expert // 2 + i, 2, 0)
    else:
        block, tiles, index = (1, LANES, depth), count, lambda i: (first_expert + i, 0, 0)
    return pl.pallas_call(
        code_kernel,
        grid=(tiles,),
        out_shape=jax.ShapeDtypeStruct((depth, 256 * tiles), jnp.bfloat16),
        in_specs=[pl.BlockSpec(block, index)] * 2,
        out_specs=pl.BlockSpec((depth, 256), lambda i: (0, i)),
        compiler_params=pltpu.CompilerParams(vmem_limit_bytes=8 << 20),
        cost_estimate=pl.CostEstimate(flops=10**9 * tiles // 2, bytes_accessed=4 * tiles * depth * 256, transcendentals=0),
        name="code",
    )(gate, up)


def hidden_kernel(*refs, count, pieces, experts):
    chunks = refs[:count]
    own = refs[count : count + pieces]
    other = refs[count + pieces : count + 2 * pieces]
    outs = refs[count + 2 * pieces : 2 * count + 2 * pieces]
    (tok,) = refs[2 * count + 2 * pieces :]
    sizes = [chunk.shape[0] for chunk in chunks]
    width = tok.shape[1]
    core = lax.axis_index("tp")
    depth = own[0].shape[0]
    total = sum(sizes)
    at = 0
    mixes = []
    for chunk, rows in zip(chunks, sizes):
        tok[at : at + rows, :] = chunk[:, :width]
        parts = chunk[:, width:].astype(jnp.float32)
        mixes.append(parts[:, :experts] + parts[:, experts : 2 * experts] + parts[:, 2 * experts : 3 * experts])
        at += rows
    mix = jnp.concatenate(mixes, axis=0) if count > 1 else mixes[0]
    near = tok[:, pl.ds(pl.multiple_of(core * depth, LANES), depth)]
    far = tok[:, pl.ds(pl.multiple_of((1 - core) * depth, LANES), depth)]
    lane = lax.broadcasted_iota(jnp.int32, (total, LANES), 1)
    first_sum = jnp.zeros((total, LANES), jnp.float32)
    second_sum = jnp.zeros((total, LANES), jnp.float32)
    per_piece = own[0].shape[1] // 256
    for tile in range(per_piece * pieces):
        piece, inside = divmod(tile, per_piece)
        columns = slice(inside * 256, inside * 256 + 256)
        both = jnp.dot(near, own[piece][:, columns], preferred_element_type=jnp.float32)
        both += jnp.dot(far, other[piece][:, columns], preferred_element_type=jnp.float32)
        gate = jnp.minimum(both[:, :LANES], LIMIT)
        up = jnp.clip(both[:, LANES:], -LIMIT, LIMIT)
        active = gate * jax.nn.sigmoid(1.702 * gate) * (up + 1.0)
        active = active.astype(jnp.bfloat16).astype(jnp.float32)
        if tile < experts:
            first_sum += active * mix[:, tile : tile + 1]
        else:
            pair = 2 * (tile - experts)
            second_sum += active * jnp.where(lane < LANES // 2, mix[:, pair : pair + 1], mix[:, pair + 1 : pair + 2])
    last = second_sum[:, : LANES // 2] + second_sum[:, LANES // 2 :]
    at = 0
    for out, rows in zip(outs, sizes):
        out[:, :LANES] = first_sum[at : at + rows].astype(jnp.bfloat16)
        out[:, LANES:] = last[at : at + rows].astype(jnp.bfloat16)
        at += rows


def hidden_units(chunks, own, other, experts):
    units = 3 * LANES // 2
    sizes = [chunk.shape[0] for chunk in chunks]
    total, width = sum(sizes), 2 * own[0].shape[0]
    return pl.pallas_call(
        functools.partial(hidden_kernel, count=len(chunks), pieces=len(own), experts=experts),
        out_shape=[jax.ShapeDtypeStruct((rows, units), jnp.bfloat16) for rows in sizes],
        in_specs=[pl.BlockSpec(memory_space=pltpu.VMEM)] * (len(chunks) + 2 * len(own)),
        out_specs=[pl.BlockSpec(memory_space=pltpu.VMEM)] * len(chunks),
        scratch_shapes=[pltpu.VMEM((total, width), jnp.bfloat16)],
        compiler_params=pltpu.CompilerParams(vmem_limit_bytes=20 << 20),
        cost_estimate=pl.CostEstimate(
            flops=2 * 3 * experts * LANES * width * max(total, 256), bytes_accessed=0, transcendentals=0
        ),
        name="hidden",
    )(*chunks, *own, *other)


def join_kernel(*refs, steps):
    blocks, out_ref, held = refs[: len(steps)], refs[len(steps)], refs[len(steps) + 1]
    owners = lax.axis_size("ep")
    place = ring_place(lax.axis_index("ep"), owners)
    units = blocks[0].shape[1]
    for block, step in zip(blocks, steps):
        held[ring_owner((place + step + owners) % owners, owners)] = block[...]
    for owner in range(owners):
        out_ref[:, owner * units : (owner + 1) * units] = held[owner]


def join_units(blocks, steps):
    rows, units = blocks[0].shape
    return pl.pallas_call(
        functools.partial(join_kernel, steps=steps),
        out_shape=jax.ShapeDtypeStruct((rows, units * len(steps)), jnp.bfloat16),
        in_specs=[pl.BlockSpec(memory_space=pltpu.VMEM)] * len(blocks),
        out_specs=pl.BlockSpec(memory_space=pltpu.VMEM),
        scratch_shapes=[pltpu.VMEM((len(steps), rows, units), jnp.bfloat16)],
        name="join",
    )(*blocks)


def pack_kernel(tokens_ref, ids_ref, weights_ref, out_ref, *, experts):
    rows, width = tokens_ref.shape
    out_ref[:, :width] = tokens_ref[...]
    number = lax.broadcasted_iota(jnp.int32, (experts, rows), 0)
    mix = jnp.zeros((experts, rows), jnp.float32)
    for choice in range(ids_ref.shape[0]):
        mix += jnp.where(ids_ref[choice : choice + 1, :] == number, weights_ref[choice : choice + 1, :], 0.0)
    high = mix.astype(jnp.bfloat16).astype(jnp.float32)
    middle = (mix - high).astype(jnp.bfloat16).astype(jnp.float32)
    low = mix - high - middle
    fill = jnp.zeros((LANES - 3 * experts, rows), jnp.float32)
    out_ref[:, width:] = jnp.concatenate([high, middle, low, fill], axis=0).T.astype(jnp.bfloat16)


def pack_tokens(tokens, expert_ids, combine_weights, experts):
    rows, width = tokens.shape
    return pl.pallas_call(
        functools.partial(pack_kernel, experts=experts),
        out_shape=jax.ShapeDtypeStruct((rows, width + LANES), jnp.bfloat16),
        in_specs=[pl.BlockSpec(memory_space=pltpu.VMEM)] * 3,
        out_specs=pl.BlockSpec(memory_space=pltpu.VMEM),
        name="pack",
    )(tokens, expert_ids.T, combine_weights.T)


def resident(tokens, expert_ids, combine_weights, gate_weight, up_weight):
    experts = gate_weight.shape[0]
    owners = lax.axis_size("ep")
    rows = tokens.shape[0]
    half = rows // 2
    tie = lax.optimization_barrier

    def swap(part):
        return lax.ppermute(part, "tp", [(0, 1), (1, 0)])

    def onward(right, left):
        return ring_send(right, owners, 1), ring_send(left, owners, -1)

    packed = pack_tokens(tokens, expert_ids, combine_weights, experts)
    packed, gate_weight, up_weight = tie((packed, gate_weight, up_weight))
    right1, left1 = onward(packed, packed)
    own = [code_weights(gate_weight, up_weight, 0, experts // 2, False)]
    own.append(code_weights(gate_weight, up_weight, experts // 2, experts // 2, False))

    right1, left1, own, gate_weight, up_weight = tie((right1, left1, own, gate_weight, up_weight))
    right2, left2 = onward(right1, left1)
    other = [swap(part) for part in own]
    own.append(code_weights(gate_weight, up_weight, 0, experts, True))

    right2, left2, own = tie((right2, left2, own))
    right3, left3 = onward(right2, left2)
    other.append(swap(own[2]))
    home, from1, back1, from2, back2 = hidden_units([packed, right1, left1, right2, left2], own, other, experts)

    right3, left3, from1, back1, from2, back2 = tie((right3, left3, from1, back1, from2, back2))
    right4, left4 = onward(right3[:half], left3[half:])
    done = {0: home}
    for step, value in ((1, from1), (-1, back1), (2, from2), (-2, back2)):
        done[step] = ring_send(value, owners, -step)
    from3, back3, *ends = hidden_units([right3, left3, right4, left4], own, other, experts)
    for step, value in ((4, jnp.concatenate(ends, axis=0)), (3, from3), (-3, back3)):
        done[step] = ring_send(value, owners, -step)
    places = tuple(sorted(done))
    return join_units([done[p] for p in places], places)


def block_scale(largest):
    scale = jnp.full(largest.shape, 2.0 ** (-40), jnp.float32)
    for exponent_value in range(-39, 9):
        power = 2.0**exponent_value
        scale = jnp.where(largest >= power, jnp.float32(power), scale)
    return scale * 0.25


def code_blocks(weight):
    shaped = weight.reshape(weight.shape[:-1] + (weight.shape[-1] // 32, 32))
    magnitude = jnp.abs(shaped).astype(jnp.float32)
    scale = block_scale(jnp.max(magnitude, axis=-1))[..., None]
    total = jnp.zeros(magnitude.shape, jnp.float32)
    for bound_value, step_value in zip(THRESHOLDS, STEPS_UP):
        total = total + jnp.where(magnitude > bound_value * scale, step_value, 0.0)
    signed = jnp.where(shaped < 0, -total, total) * scale
    return signed.reshape(weight.shape).astype(jnp.bfloat16)


def activate(gate_value, up_value):
    gate_clamped = jnp.minimum(gate_value, LIMIT)
    up_clamped = jnp.clip(up_value, -LIMIT, LIMIT)
    return gate_clamped * jax.nn.sigmoid(1.702 * gate_clamped) * (up_clamped + 1.0)


def dispatched(tokens, expert_ids, combine_weights, gate_weight, up_weight):
    experts = gate_weight.shape[0]
    owners = lax.axis_size("ep")
    cores = lax.axis_size("tp")
    tok_rows = tokens.shape[0]
    top_count = expert_ids.shape[1]
    width = tokens.shape[1]
    slots = max(2, 2 * tok_rows * top_count // experts)
    gate_split, up_split = (
        lax.all_to_all(gate_weight, "tp", split_axis=1, concat_axis=2, tiled=True),
        lax.all_to_all(up_weight, "tp", split_axis=1, concat_axis=2, tiled=True),
    )
    gate_local, up_local = (
        lax.all_to_all(gate_split, "ep", split_axis=0, concat_axis=1, tiled=True),
        lax.all_to_all(up_split, "ep", split_axis=0, concat_axis=1, tiled=True),
    )
    gate_coded = code_blocks(gate_local[0])
    up_coded = code_blocks(up_local[0])
    chosen = expert_ids.reshape(-1)
    onehot = (chosen[:, None] == jnp.arange(experts, dtype=jnp.int32)[None, :]).astype(jnp.int32)
    before = jnp.cumsum(onehot, axis=0, dtype=jnp.int32) - onehot
    ranking = jnp.sum(before * onehot, axis=1, dtype=jnp.int32)
    target = chosen * slots + ranking
    repeated = jnp.repeat(tokens, top_count, axis=0)
    outgoing = jnp.zeros((experts * slots, width), jnp.bfloat16).at[target].set(repeated)
    received = lax.all_to_all(
        outgoing.reshape(experts, slots, width), "ep", split_axis=0, concat_axis=0, tiled=True
    )
    piece = lax.all_gather(received.reshape(owners * slots, width), "tp", axis=0, tiled=True)
    gate_value = jnp.einsum("rd,fd->rf", piece, gate_coded, preferred_element_type=jnp.float32)
    up_value = jnp.einsum("rd,fd->rf", piece, up_coded, preferred_element_type=jnp.float32)
    actives = activate(gate_value, up_value).astype(jnp.bfloat16)
    shaped_back = actives.reshape(cores, owners, slots, actives.shape[1])
    returned = lax.all_to_all(
        lax.all_to_all(shaped_back, "ep", split_axis=1, concat_axis=1, tiled=True),
        "tp",
        split_axis=0,
        concat_axis=3,
        tiled=True,
    )
    flat_back = returned.reshape(experts * slots, returned.shape[3])
    values = flat_back[target].reshape(tok_rows, top_count, flat_back.shape[1])
    mixed = jnp.einsum("tk,tkf->tf", combine_weights, values.astype(jnp.float32))
    hidden_total = mixed.shape[1]
    quarter = hidden_total // (owners * cores)
    mixed = (
        mixed.reshape(tok_rows, cores, owners, quarter)
        .transpose(0, 2, 1, 3)
        .reshape(tok_rows, hidden_total)
    )
    return mixed.astype(jnp.bfloat16)


def per_device(tokens, expert_ids, combine_weights, gate_weight, up_weight):
    experts, units, depth = gate_weight.shape
    owners, cores = lax.axis_size("ep"), lax.axis_size("tp")
    fits = owners == 8 and cores == 2 and experts <= 4 * expert_ids.shape[1] and experts % 8 == 0
    fits = fits and units == 3 * LANES // 2 and depth % 256 == 0 and tokens.shape[0] % 64 == 0
    plan = resident if fits else dispatched
    return plan(tokens, expert_ids, combine_weights, gate_weight, up_weight)


def solution(mesh):
    return jax.shard_map(
        per_device,
        mesh=mesh,
        in_specs=(
            P(("groups", "ep", "tp"), None),
            P(("groups", "ep", "tp"), None),
            P(("groups", "ep", "tp"), None),
            P(None, "ep", "tp"),
            P(None, "ep", "tp"),
        ),
        out_specs=P(("groups", "ep", "tp"), None),
        check_vma=False,
    )
```

```python
import functools

import jax
import jax.numpy as jnp
from jax import lax
from jax.experimental import pallas as pl
from jax.experimental.pallas import tpu as pltpu
from jax.sharding import PartitionSpec as P

THRESHOLDS = (0.25, 0.75, 1.25, 1.75, 2.5, 3.5, 5.0)
STEPS_UP = (0.5, 0.5, 0.5, 0.5, 1.0, 1.0, 2.0)
LIMIT = 7.0
LANES = 128
BLOCK = 32


def ring_place(owner, owners):
    return jnp.where(owner % 2 == 0, owner // 2, owners - 1 - owner // 2)


def ring_owner(place, owners):
    return jnp.where(place < owners // 2, 2 * place, 2 * (owners - 1 - place) + 1)


def ring_shift(owners, steps):
    order = list(range(0, owners, 2)) + list(range(1, owners, 2))[::-1]
    return [(order[p], order[(p + steps) % owners]) for p in range(owners)]


def ring_send(value, owners, steps):
    return lax.ppermute(value, "ep", ring_shift(owners, steps))


def code_columns(entries):
    depth, count = entries.shape
    blocks = entries.reshape(depth // BLOCK, BLOCK, count)
    largest = jnp.max(jnp.abs(blocks), axis=1, keepdims=True)
    largest = jnp.maximum(largest, 2.0**-40)
    lifted = largest * 2.0**23
    power = jnp.minimum((largest * 0.7 + lifted) - lifted, 2.0**8)
    lowered = blocks * (1.0 - 2.0**-12)
    top = power * 1.5
    lowered = jnp.minimum(jnp.maximum(lowered, -top), top)
    least = power * (0.25 * (1.0 + 2.0**-10))
    anchor = jnp.maximum(jnp.abs(lowered), least) * 2.0**22
    return ((lowered + anchor) - anchor).reshape(depth, count)


def tile_rows(tile, experts):
    if tile < experts:
        return [(tile, 0, LANES)]
    pair = 2 * (tile - experts)
    return [(pair, LANES, LANES // 2), (pair + 1, LANES, LANES // 2)]


def code_tile(rows_ref, out_ref, first):
    depth = rows_ref.shape[1]
    for low in range(0, depth, 256):
        turned = rows_ref[:, low : low + 256].T.astype(jnp.float32)
        out_ref[low : low + 256, pl.ds(first, 256)] = code_columns(turned).astype(jnp.bfloat16)


def fetch_rows(gate_ref, up_ref, tiles, target, arrived):
    experts = gate_ref.shape[0]
    groups = []
    for n, tile in enumerate(tiles):
        group, at = [], 0
        for ref in (gate_ref, up_ref):
            for expert, first, count in tile_rows(tile, experts):
                source = ref.at[expert, first : first + count]
                group.append(pltpu.make_async_copy(source, target.at[n, at : at + count], arrived.at[n, len(group)]))
                at += count
        groups.append(group)
    return groups


def code_kernel(*refs, following):
    if following:
        gate_ref, up_ref, rows_ref, _, out_ref, rest_ref, arrived = refs
        groups = fetch_rows(gate_ref, up_ref, following, rest_ref, arrived)
    else:
        (rows_ref, _, out_ref), groups = refs, []
    for group in groups:
        for copy in group:
            copy.start()

    @pl.loop(0, rows_ref.shape[0])
    def _(n):
        code_tile(rows_ref.at[n], out_ref, pl.multiple_of(n * 256, 256))

    for group in groups:
        for copy in group:
            copy.wait()


def code_weights(gate, up, rows, following, after):
    tiles, _, depth = rows.shape
    outs = [pltpu.VMEM((depth, 256 * tiles), jnp.bfloat16)]
    operands, scratch = [rows, after], []
    spaces = [pltpu.VMEM, pl.ANY]
    if following:
        outs.append(pltpu.VMEM((len(following), 2 * LANES, depth), jnp.bfloat16))
        operands = [pltpu.with_memory_space_constraint(x, pltpu.HBM) for x in (gate, up)] + operands
        spaces = [pl.ANY, pl.ANY] + spaces
        scratch = [pltpu.SemaphoreType.DMA((len(following), 4))]
    return pl.pallas_call(
        functools.partial(code_kernel, following=following),
        out_shape=outs,
        in_specs=[pl.BlockSpec(memory_space=space) for space in spaces],
        out_specs=[pl.BlockSpec(memory_space=pltpu.VMEM)] * len(outs),
        scratch_shapes=scratch,
        compiler_params=pltpu.CompilerParams(vmem_limit_bytes=12 << 20),
        cost_estimate=pl.CostEstimate(flops=1024, bytes_accessed=1024, transcendentals=0),
        name="code",
    )(*operands)


def begin_kernel(
    tokens_ref, ids_ref, weights_ref, gate_ref, up_ref, packed_ref, out_ref, rest_ref, ids, weights, held, near, fetched,
    *, tiles, following,
):
    experts = gate_ref.shape[0]
    rows, width = tokens_ref.shape
    routes = [
        pltpu.make_async_copy(ids_ref, ids, near.at[0]),
        pltpu.make_async_copy(weights_ref, weights, near.at[1]),
    ]
    moved = pltpu.make_async_copy(tokens_ref, packed_ref.at[:, :width], near.at[2])
    now = len(tiles)
    groups = fetch_rows(gate_ref, up_ref, tiles, held, fetched)
    later = fetch_rows(gate_ref, up_ref, following, rest_ref, fetched.at[now:])
    for copy in routes + [moved]:
        copy.start()
    for group in groups + later:
        for copy in group:
            copy.start()
    for copy in routes:
        copy.wait()
    number = lax.broadcasted_iota(jnp.int32, (experts, rows), 0)
    mix = jnp.zeros((experts, rows), jnp.float32)
    for choice in range(ids_ref.shape[0]):
        mix += jnp.where(ids[choice : choice + 1, :] == number, weights[choice : choice + 1, :], 0.0)
    high = mix.astype(jnp.bfloat16).astype(jnp.float32)
    middle = (mix - high).astype(jnp.bfloat16).astype(jnp.float32)
    low = mix - high - middle
    fill = jnp.zeros((LANES - 3 * experts, rows), jnp.float32)
    packed_ref[:, width:] = jnp.concatenate([high, middle, low, fill], axis=0).T.astype(jnp.bfloat16)
    for n, group in enumerate(groups):
        for copy in group:
            copy.wait()
        code_tile(held.at[n], out_ref, 256 * n)
    for group in later:
        for copy in group:
            copy.wait()
    moved.wait()


def begin(tokens, expert_ids, combine_weights, gate, up, tiles, following):
    depth = gate.shape[2]
    rows, width = tokens.shape
    choices = expert_ids.shape[1]
    operands = (tokens, expert_ids.T, combine_weights.T, gate, up)
    return pl.pallas_call(
        functools.partial(begin_kernel, tiles=tiles, following=following),
        out_shape=[
            pltpu.VMEM((rows, width + LANES), jnp.bfloat16),
            pltpu.VMEM((depth, 256 * len(tiles)), jnp.bfloat16),
            pltpu.VMEM((len(following), 2 * LANES, depth), jnp.bfloat16),
        ],
        in_specs=[pl.BlockSpec(memory_space=pl.ANY)] * 5,
        out_specs=[pl.BlockSpec(memory_space=pltpu.VMEM)] * 3,
        scratch_shapes=[
            pltpu.VMEM((choices, rows), jnp.int32),
            pltpu.VMEM((choices, rows), jnp.float32),
            pltpu.VMEM((len(tiles), 2 * LANES, depth), jnp.bfloat16),
            pltpu.SemaphoreType.DMA((3,)),
            pltpu.SemaphoreType.DMA((len(tiles) + len(following), 4)),
        ],
        compiler_params=pltpu.CompilerParams(vmem_limit_bytes=16 << 20),
        cost_estimate=pl.CostEstimate(flops=1024, bytes_accessed=1024, transcendentals=0),
        name="begin",
    )(*(pltpu.with_memory_space_constraint(x, pltpu.HBM) for x in operands))


def hidden_kernel(*refs, count, pieces, after, experts):
    chunks = refs[:count]
    own = refs[count : count + pieces]
    other = refs[count + pieces : count + 2 * pieces]
    *outs, tok = refs[count + 2 * pieces + after :]
    sizes = [chunk.shape[0] for chunk in chunks]
    width = tok.shape[1]
    core = lax.axis_index("tp")
    depth = own[0].shape[0]
    total = sum(sizes)
    at = 0
    mixes = []
    for chunk, rows in zip(chunks, sizes):
        tok[at : at + rows, :] = chunk[:, :width]
        parts = chunk[:, width:].astype(jnp.float32)
        mixes.append(parts[:, :experts] + parts[:, experts : 2 * experts] + parts[:, 2 * experts : 3 * experts])
        at += rows
    mix = jnp.concatenate(mixes, axis=0) if count > 1 else mixes[0]
    near = tok[:, pl.ds(pl.multiple_of(core * depth, LANES), depth)]
    far = tok[:, pl.ds(pl.multiple_of((1 - core) * depth, LANES), depth)]
    lane = lax.broadcasted_iota(jnp.int32, (total, LANES), 1)
    first_sum = jnp.zeros((total, LANES), jnp.float32)
    second_sum = jnp.zeros((total, LANES), jnp.float32)
    places = [(piece, at) for piece in range(pieces) for at in range(0, own[piece].shape[1], 256)]
    for tile, (piece, at) in enumerate(places):
        columns = slice(at, at + 256)
        both = jnp.dot(near, own[piece][:, columns], preferred_element_type=jnp.float32)
        both += jnp.dot(far, other[piece][:, columns], preferred_element_type=jnp.float32)
        gate = jnp.minimum(both[:, :LANES], LIMIT)
        up = jnp.clip(both[:, LANES:], -LIMIT, LIMIT)
        active = gate * jax.nn.sigmoid(1.702 * gate) * (up + 1.0)
        active = active.astype(jnp.bfloat16).astype(jnp.float32)
        if tile < experts:
            first_sum += active * mix[:, tile : tile + 1]
        else:
            pair = 2 * (tile - experts)
            second_sum += active * jnp.where(lane < LANES // 2, mix[:, pair : pair + 1], mix[:, pair + 1 : pair + 2])
    last = second_sum[:, : LANES // 2] + second_sum[:, LANES // 2 :]
    at = 0
    for out, rows in zip(outs, sizes):
        out[:, :LANES] = first_sum[at : at + rows].astype(jnp.bfloat16)
        out[:, LANES:] = last[at : at + rows].astype(jnp.bfloat16)
        at += rows


def hidden_units(chunks, own, other, experts, *after):
    units = 3 * LANES // 2
    sizes = [chunk.shape[0] for chunk in chunks]
    total, width = sum(sizes), 2 * own[0].shape[0]
    return pl.pallas_call(
        functools.partial(hidden_kernel, count=len(chunks), pieces=len(own), after=len(after), experts=experts),
        out_shape=[jax.ShapeDtypeStruct((rows, units), jnp.bfloat16) for rows in sizes],
        in_specs=[pl.BlockSpec(memory_space=pltpu.VMEM)] * (len(chunks) + 2 * len(own))
        + [pl.BlockSpec(memory_space=pl.ANY)] * len(after),
        out_specs=[pl.BlockSpec(memory_space=pltpu.VMEM)] * len(chunks),
        scratch_shapes=[pltpu.VMEM((total, width), jnp.bfloat16)],
        compiler_params=pltpu.CompilerParams(vmem_limit_bytes=20 << 20),
        cost_estimate=pl.CostEstimate(flops=12*10**9, bytes_accessed=1024, transcendentals=0),
        name="hidden",
    )(*chunks, *own, *other, *after)


def join_kernel(*refs, steps):
    blocks, out_ref, held = refs[: len(steps)], refs[len(steps)], refs[len(steps) + 1]
    owners = lax.axis_size("ep")
    place = ring_place(lax.axis_index("ep"), owners)
    units = blocks[0].shape[1]
    for block, step in zip(blocks, steps):
        held[ring_owner((place + step + owners) % owners, owners)] = block[...]
    for owner in range(owners):
        out_ref[:, owner * units : (owner + 1) * units] = held[owner]


def join_units(blocks, steps):
    rows, units = blocks[0].shape
    return pl.pallas_call(
        functools.partial(join_kernel, steps=steps),
        out_shape=jax.ShapeDtypeStruct((rows, units * len(steps)), jnp.bfloat16),
        in_specs=[pl.BlockSpec(memory_space=pltpu.VMEM)] * len(blocks),
        out_specs=pl.BlockSpec(memory_space=pltpu.VMEM),
        scratch_shapes=[pltpu.VMEM((len(steps), rows, units), jnp.bfloat16)],
        compiler_params=pltpu.CompilerParams(vmem_limit_bytes=4 << 20),
        name="join",
    )(*blocks)


def mark_kernel(*refs):
    refs[-1][...] = jnp.zeros(refs[-1].shape, refs[-1].dtype)


def mark(*after):
    return pl.pallas_call(
        mark_kernel,
        out_shape=jax.ShapeDtypeStruct((8, LANES), jnp.float32),
        in_specs=[pl.BlockSpec(memory_space=pl.ANY)] * len(after),
        out_specs=pl.BlockSpec(memory_space=pltpu.VMEM),
        compiler_params=pltpu.CompilerParams(vmem_limit_bytes=1 << 20),
        cost_estimate=pl.CostEstimate(flops=6*10**10, bytes_accessed=1024, transcendentals=0),
        name="mark",
    )(*after)


def resident(tokens, expert_ids, combine_weights, gate_weight, up_weight):
    experts = gate_weight.shape[0]
    owners = lax.axis_size("ep")
    rows = tokens.shape[0]
    half = rows // 2
    tie = lax.optimization_barrier

    def swap(part):
        return lax.ppermute(part, "tp", [(0, 1), (1, 0)])

    def onward(right, left):
        return ring_send(right, owners, 1), ring_send(left, owners, -1)

    tiles = tuple(range(experts * 3 // 2))
    now, soon, later = tiles[:3], tiles[3:7], tiles[7:]
    packed, first, rest = begin(tokens, expert_ids, combine_weights, gate_weight, up_weight, now, soon)
    right1, left1 = onward(packed, packed)
    own, other = [first], [swap(first)]
    coded, rest = code_weights(gate_weight, up_weight, rest, later, other[0])
    own.append(coded)
    own += code_weights(gate_weight, up_weight, rest, (), coded)
    other += [swap(part) for part in own[1:]]

    right1, left1, point = tie((right1, left1, mark(right1, left1, own[2])))
    right2, left2 = onward(right1, left1)
    home, from1, back1 = hidden_units([packed, right1, left1], own, other, experts, point)
    done = {0: home, 1: ring_send(from1, owners, -1), -1: ring_send(back1, owners, 1)}

    right2, left2, _ = tie((right2, left2, from1))
    right3, left3 = onward(right2, left2)
    from2, back2 = hidden_units([right2, left2], own, other, experts, done[1], done[-1])
    done[2], done[-2] = ring_send(from2, owners, -2), ring_send(back2, owners, 2)

    right3, left3, _ = tie((right3, left3, from2))
    right4, left4 = onward(right3[:half], left3[half:])
    from3, back3 = hidden_units([right3, left3], own, other, experts, done[2], done[-2])
    done[3], done[-3] = ring_send(from3, owners, -3), ring_send(back3, owners, 3)

    right4, left4, _ = tie((right4, left4, from3))
    ends = hidden_units([right4, left4], own, other, experts)
    done[4] = ring_send(jnp.concatenate(ends, axis=0), owners, 4)
    places = tuple(sorted(done))
    return join_units([done[p] for p in places], places)


def block_scale(largest):
    scale = jnp.full(largest.shape, 2.0 ** (-40), jnp.float32)
    for exponent_value in range(-39, 9):
        power = 2.0**exponent_value
        scale = jnp.where(largest >= power, jnp.float32(power), scale)
    return scale * 0.25


def code_blocks(weight):
    shaped = weight.reshape(weight.shape[:-1] + (weight.shape[-1] // 32, 32))
    magnitude = jnp.abs(shaped).astype(jnp.float32)
    scale = block_scale(jnp.max(magnitude, axis=-1))[..., None]
    total = jnp.zeros(magnitude.shape, jnp.float32)
    for bound_value, step_value in zip(THRESHOLDS, STEPS_UP):
        total = total + jnp.where(magnitude > bound_value * scale, step_value, 0.0)
    signed = jnp.where(shaped < 0, -total, total) * scale
    return signed.reshape(weight.shape).astype(jnp.bfloat16)


def activate(gate_value, up_value):
    gate_clamped = jnp.minimum(gate_value, LIMIT)
    up_clamped = jnp.clip(up_value, -LIMIT, LIMIT)
    return gate_clamped * jax.nn.sigmoid(1.702 * gate_clamped) * (up_clamped + 1.0)


def dispatched(tokens, expert_ids, combine_weights, gate_weight, up_weight):
    experts = gate_weight.shape[0]
    owners = lax.axis_size("ep")
    cores = lax.axis_size("tp")
    tok_rows = tokens.shape[0]
    top_count = expert_ids.shape[1]
    width = tokens.shape[1]
    slots = max(2, 2 * tok_rows * top_count // experts)
    gate_split, up_split = (
        lax.all_to_all(gate_weight, "tp", split_axis=1, concat_axis=2, tiled=True),
        lax.all_to_all(up_weight, "tp", split_axis=1, concat_axis=2, tiled=True),
    )
    gate_local, up_local = (
        lax.all_to_all(gate_split, "ep", split_axis=0, concat_axis=1, tiled=True),
        lax.all_to_all(up_split, "ep", split_axis=0, concat_axis=1, tiled=True),
    )
    gate_coded = code_blocks(gate_local[0])
    up_coded = code_blocks(up_local[0])
    chosen = expert_ids.reshape(-1)
    onehot = (chosen[:, None] == jnp.arange(experts, dtype=jnp.int32)[None, :]).astype(jnp.int32)
    before = jnp.cumsum(onehot, axis=0, dtype=jnp.int32) - onehot
    ranking = jnp.sum(before * onehot, axis=1, dtype=jnp.int32)
    target = chosen * slots + ranking
    repeated = jnp.repeat(tokens, top_count, axis=0)
    outgoing = jnp.zeros((experts * slots, width), jnp.bfloat16).at[target].set(repeated)
    received = lax.all_to_all(
        outgoing.reshape(experts, slots, width), "ep", split_axis=0, concat_axis=0, tiled=True
    )
    piece = lax.all_gather(received.reshape(owners * slots, width), "tp", axis=0, tiled=True)
    gate_value = jnp.einsum("rd,fd->rf", piece, gate_coded, preferred_element_type=jnp.float32)
    up_value = jnp.einsum("rd,fd->rf", piece, up_coded, preferred_element_type=jnp.float32)
    actives = activate(gate_value, up_value).astype(jnp.bfloat16)
    shaped_back = actives.reshape(cores, owners, slots, actives.shape[1])
    returned = lax.all_to_all(
        lax.all_to_all(shaped_back, "ep", split_axis=1, concat_axis=1, tiled=True),
        "tp",
        split_axis=0,
        concat_axis=3,
        tiled=True,
    )
    flat_back = returned.reshape(experts * slots, returned.shape[3])
    values = flat_back[target].reshape(tok_rows, top_count, flat_back.shape[1])
    mixed = jnp.einsum("tk,tkf->tf", combine_weights, values.astype(jnp.float32))
    hidden_total = mixed.shape[1]
    quarter = hidden_total // (owners * cores)
    mixed = (
        mixed.reshape(tok_rows, cores, owners, quarter)
        .transpose(0, 2, 1, 3)
        .reshape(tok_rows, hidden_total)
    )
    return mixed.astype(jnp.bfloat16)


def per_device(tokens, expert_ids, combine_weights, gate_weight, up_weight):
    experts, units, depth = gate_weight.shape
    owners, cores = lax.axis_size("ep"), lax.axis_size("tp")
    fits = owners == 8 and cores == 2 and experts <= 4 * expert_ids.shape[1] and experts % 8 == 0
    fits = fits and units == 3 * LANES // 2 and depth % 256 == 0 and tokens.shape[0] % 64 == 0
    plan = resident if fits else dispatched
    return plan(tokens, expert_ids, combine_weights, gate_weight, up_weight)


def solution(mesh):
    return jax.shard_map(
        per_device,
        mesh=mesh,
        in_specs=(
            P(("groups", "ep", "tp"), None),
            P(("groups", "ep", "tp"), None),
            P(("groups", "ep", "tp"), None),
            P(None, "ep", "tp"),
            P(None, "ep", "tp"),
        ),
        out_specs=P(("groups", "ep", "tp"), None),
        check_vma=False,
    )
```

```python
import functools

import jax
import jax.numpy as jnp
from jax import lax
from jax.experimental import pallas as pl
from jax.experimental.pallas import tpu as pltpu
from jax.sharding import PartitionSpec as P

THRESHOLDS = (0.25, 0.75, 1.25, 1.75, 2.5, 3.5, 5.0)
STEPS_UP = (0.5, 0.5, 0.5, 0.5, 1.0, 1.0, 2.0)
LIMIT = 7.0
LANES = 128
BLOCK = 32


def ring_place(owner, owners):
    return jnp.where(owner % 2 == 0, owner // 2, owners - 1 - owner // 2)


def ring_owner(place, owners):
    return jnp.where(place < owners // 2, 2 * place, 2 * (owners - 1 - place) + 1)


def ring_send(value, owners, steps):
    order = list(range(0, owners, 2)) + list(range(1, owners, 2))[::-1]
    pairs = [
        (2 * order[p] + core, 2 * order[(p + sign * steps) % owners] + core)
        for core, sign in ((0, 1), (1, -1))
        for p in range(owners)
    ]
    return lax.ppermute(value, ("ep", "tp"), pairs)


def code_columns(entries):
    depth, count = entries.shape
    blocks = entries.reshape(depth // BLOCK, BLOCK, count)
    largest = jnp.max(jnp.abs(blocks), axis=1, keepdims=True)
    largest = jnp.maximum(largest, 2.0**-40)
    lifted = largest * 2.0**23
    power = jnp.minimum((largest * 0.7 + lifted) - lifted, 2.0**8)
    lowered = blocks * (1.0 - 2.0**-12)
    top = power * 1.5
    lowered = jnp.minimum(jnp.maximum(lowered, -top), top)
    least = power * (0.25 * (1.0 + 2.0**-10))
    anchor = jnp.maximum(jnp.abs(lowered), least) * 2.0**22
    return ((lowered + anchor) - anchor).reshape(depth, count)


def tile_rows(tile, experts):
    if tile < experts:
        return [(tile, 0, LANES)]
    pair = 2 * (tile - experts)
    return [(pair, LANES, LANES // 2), (pair + 1, LANES, LANES // 2)]


def code_tile(rows_ref, out_ref, first):
    depth = rows_ref.shape[1]
    for low in range(0, depth, 256):
        turned = rows_ref[:, low : low + 256].T.astype(jnp.float32)
        out_ref[low : low + 256, pl.ds(first, 256)] = code_columns(turned).astype(jnp.bfloat16)


def fetch_rows(gate_ref, up_ref, tiles, target, arrived):
    experts = gate_ref.shape[0]
    groups = []
    for n, tile in enumerate(tiles):
        group, at = [], 0
        for ref in (gate_ref, up_ref):
            for expert, first, count in tile_rows(tile, experts):
                source = ref.at[expert, first : first + count]
                group.append(pltpu.make_async_copy(source, target.at[n, at : at + count], arrived.at[n, len(group)]))
                at += count
        groups.append(group)
    return groups


def code_kernel(*refs, following):
    if following:
        gate_ref, up_ref, rows_ref, _, out_ref, rest_ref, arrived = refs
        groups = fetch_rows(gate_ref, up_ref, following, rest_ref, arrived)
    else:
        (rows_ref, _, out_ref), groups = refs, []
    for group in groups:
        for copy in group:
            copy.start()

    @pl.loop(0, rows_ref.shape[0])
    def _(n):
        code_tile(rows_ref.at[n], out_ref, pl.multiple_of(n * 256, 256))

    for group in groups:
        for copy in group:
            copy.wait()


def code_weights(gate, up, rows, following, after):
    tiles, _, depth = rows.shape
    outs = [pltpu.VMEM((depth, 256 * tiles), jnp.bfloat16)]
    operands, scratch = [rows, after], []
    spaces = [pltpu.VMEM, pl.ANY]
    if following:
        outs.append(pltpu.VMEM((len(following), 2 * LANES, depth), jnp.bfloat16))
        operands = [pltpu.with_memory_space_constraint(x, pltpu.HBM) for x in (gate, up)] + operands
        spaces = [pl.ANY, pl.ANY] + spaces
        scratch = [pltpu.SemaphoreType.DMA((len(following), 4))]
    return pl.pallas_call(
        functools.partial(code_kernel, following=following),
        out_shape=outs,
        in_specs=[pl.BlockSpec(memory_space=space) for space in spaces],
        out_specs=[pl.BlockSpec(memory_space=pltpu.VMEM)] * len(outs),
        scratch_shapes=scratch,
        compiler_params=pltpu.CompilerParams(vmem_limit_bytes=12 << 20),
        cost_estimate=pl.CostEstimate(flops=1024, bytes_accessed=1024, transcendentals=0),
        name="code",
    )(*operands)


def begin_kernel(
    tokens_ref, ids_ref, weights_ref, gate_ref, up_ref, packed_ref, out_ref, rest_ref, ids, weights, held, near, fetched,
    *, tiles, following,
):
    experts = gate_ref.shape[0]
    rows, width = tokens_ref.shape
    routes = [
        pltpu.make_async_copy(ids_ref, ids, near.at[0]),
        pltpu.make_async_copy(weights_ref, weights, near.at[1]),
    ]
    moved = pltpu.make_async_copy(tokens_ref, packed_ref.at[:, :width], near.at[2])
    now = len(tiles)
    groups = fetch_rows(gate_ref, up_ref, tiles, held, fetched)
    later = fetch_rows(gate_ref, up_ref, following, rest_ref, fetched.at[now:])
    for copy in routes + [moved]:
        copy.start()
    for group in groups + later:
        for copy in group:
            copy.start()
    for copy in routes:
        copy.wait()
    number = lax.broadcasted_iota(jnp.int32, (experts, rows), 0)
    mix = jnp.zeros((experts, rows), jnp.float32)
    for choice in range(ids_ref.shape[0]):
        mix += jnp.where(ids[choice : choice + 1, :] == number, weights[choice : choice + 1, :], 0.0)
    high = mix.astype(jnp.bfloat16).astype(jnp.float32)
    middle = (mix - high).astype(jnp.bfloat16).astype(jnp.float32)
    low = mix - high - middle
    fill = jnp.zeros((LANES - 3 * experts, rows), jnp.float32)
    packed_ref[:, width:] = jnp.concatenate([high, middle, low, fill], axis=0).T.astype(jnp.bfloat16)
    for n, group in enumerate(groups):
        for copy in group:
            copy.wait()
        code_tile(held.at[n], out_ref, 256 * n)
    for group in later:
        for copy in group:
            copy.wait()
    moved.wait()


def begin(tokens, expert_ids, combine_weights, gate, up, tiles, following):
    depth = gate.shape[2]
    rows, width = tokens.shape
    choices = expert_ids.shape[1]
    operands = (tokens, expert_ids.T, combine_weights.T, gate, up)
    return pl.pallas_call(
        functools.partial(begin_kernel, tiles=tiles, following=following),
        out_shape=[
            pltpu.VMEM((rows, width + LANES), jnp.bfloat16),
            pltpu.VMEM((depth, 256 * len(tiles)), jnp.bfloat16),
            pltpu.VMEM((len(following), 2 * LANES, depth), jnp.bfloat16),
        ],
        in_specs=[pl.BlockSpec(memory_space=pl.ANY)] * 5,
        out_specs=[pl.BlockSpec(memory_space=pltpu.VMEM)] * 3,
        scratch_shapes=[
            pltpu.VMEM((choices, rows), jnp.int32),
            pltpu.VMEM((choices, rows), jnp.float32),
            pltpu.VMEM((len(tiles), 2 * LANES, depth), jnp.bfloat16),
            pltpu.SemaphoreType.DMA((3,)),
            pltpu.SemaphoreType.DMA((len(tiles) + len(following), 4)),
        ],
        compiler_params=pltpu.CompilerParams(vmem_limit_bytes=16 << 20),
        cost_estimate=pl.CostEstimate(flops=1024, bytes_accessed=1024, transcendentals=0),
        name="begin",
    )(*(pltpu.with_memory_space_constraint(x, pltpu.HBM) for x in operands))


def hidden_kernel(*refs, count, pieces, after, experts):
    chunks = refs[:count]
    own = refs[count : count + pieces]
    other = refs[count + pieces : count + 2 * pieces]
    *outs, tok = refs[count + 2 * pieces + after :]
    sizes = [chunk.shape[0] for chunk in chunks]
    width = tok.shape[1]
    core = lax.axis_index("tp")
    depth = own[0].shape[0]
    total = tok.shape[0]
    at = 0
    mixes = []
    for chunk, rows in zip(chunks, sizes):
        tok[at : at + rows, :] = chunk[:, :width]
        parts = chunk[:, width : width + LANES].astype(jnp.float32)
        mixes.append(parts[:, :experts] + parts[:, experts : 2 * experts] + parts[:, 2 * experts : 3 * experts])
        at += rows
    if at < total:
        tok[at:, :] = jnp.zeros((total - at, width), tok.dtype)
        mixes.append(jnp.zeros((total - at, experts), jnp.float32))
    mix = jnp.concatenate(mixes, axis=0) if len(mixes) > 1 else mixes[0]
    near = tok[:, pl.ds(pl.multiple_of(core * depth, LANES), depth)]
    far = tok[:, pl.ds(pl.multiple_of((1 - core) * depth, LANES), depth)]
    lane = lax.broadcasted_iota(jnp.int32, (total, LANES), 1)
    first_sum = jnp.zeros((total, LANES), jnp.float32)
    second_sum = jnp.zeros((total, LANES), jnp.float32)
    places = [(piece, at) for piece in range(pieces) for at in range(0, own[piece].shape[1], 256)]
    for tile, (piece, at) in enumerate(places):
        columns = slice(at, at + 256)
        both = jnp.dot(near, own[piece][:, columns], preferred_element_type=jnp.float32)
        both += jnp.dot(far, other[piece][:, columns], preferred_element_type=jnp.float32)
        gate = jnp.minimum(both[:, :LANES], LIMIT)
        up = jnp.clip(both[:, LANES:], -LIMIT, LIMIT)
        active = gate * jax.nn.sigmoid(1.702 * gate) * (up + 1.0)
        active = active.astype(jnp.bfloat16).astype(jnp.float32)
        if tile < experts:
            first_sum += active * mix[:, tile : tile + 1]
        else:
            pair = 2 * (tile - experts)
            second_sum += active * jnp.where(lane < LANES // 2, mix[:, pair : pair + 1], mix[:, pair + 1 : pair + 2])
    last = second_sum[:, : LANES // 2] + second_sum[:, LANES // 2 :]
    at = 0
    for out, rows in zip(outs, sizes):
        out[:, :LANES] = first_sum[at : at + rows].astype(jnp.bfloat16)
        out[:, LANES:] = last[at : at + rows].astype(jnp.bfloat16)
        at += rows


def hidden_units(chunks, own, other, experts, *after):
    units = 3 * LANES // 2
    sizes = [chunk.shape[0] for chunk in chunks]
    total, width = max(sum(sizes), LANES), 2 * own[0].shape[0]
    return pl.pallas_call(
        functools.partial(hidden_kernel, count=len(chunks), pieces=len(own), after=len(after), experts=experts),
        out_shape=[jax.ShapeDtypeStruct((rows, units), jnp.bfloat16) for rows in sizes],
        in_specs=[pl.BlockSpec(memory_space=pltpu.VMEM)] * (len(chunks) + 2 * len(own))
        + [pl.BlockSpec(memory_space=pl.ANY)] * len(after),
        out_specs=[pl.BlockSpec(memory_space=pltpu.VMEM)] * len(chunks),
        scratch_shapes=[pltpu.VMEM((total, width), jnp.bfloat16)],
        compiler_params=pltpu.CompilerParams(vmem_limit_bytes=20 << 20),
        cost_estimate=pl.CostEstimate(flops=12*10**9, bytes_accessed=1024, transcendentals=0),
        name="hidden",
    )(*chunks, *own, *other, *after)


def join_kernel(*refs, steps):
    blocks, out_ref, held = refs[: len(steps)], refs[len(steps)], refs[len(steps) + 1]
    owners = lax.axis_size("ep")
    place = ring_place(lax.axis_index("ep"), owners)
    sign = 1 - 2 * lax.axis_index("tp")
    units = held.shape[2]
    for block, step in zip(blocks, steps):
        first = max(block.shape[1] - 2 * LANES, 0)
        held[ring_owner((place + sign * step + owners) % owners, owners)] = block[:, first : first + units]
    for owner in range(owners):
        out_ref[:, owner * units : (owner + 1) * units] = held[owner]


def join_units(blocks, steps, units):
    rows = blocks[0].shape[0]
    return pl.pallas_call(
        functools.partial(join_kernel, steps=steps),
        out_shape=jax.ShapeDtypeStruct((rows, units * len(steps)), jnp.bfloat16),
        in_specs=[pl.BlockSpec(memory_space=pltpu.VMEM)] * len(blocks),
        out_specs=pl.BlockSpec(memory_space=pltpu.VMEM),
        scratch_shapes=[pltpu.VMEM((len(steps), rows, units), jnp.bfloat16)],
        compiler_params=pltpu.CompilerParams(vmem_limit_bytes=4 << 20),
        name="join",
    )(*blocks)


def attach_kernel(chunk_ref, block_ref, out_ref):
    width, units = chunk_ref.shape[1], block_ref.shape[1]
    out_ref[:, :width] = chunk_ref[...]
    out_ref[:, width : width + units] = block_ref[...]
    out_ref[:, width + units :] = jnp.zeros((out_ref.shape[0], 2 * LANES - units), out_ref.dtype)


def attach(chunk, block):
    rows, width = chunk.shape
    return pl.pallas_call(
        attach_kernel,
        out_shape=jax.ShapeDtypeStruct((rows, width + 2 * LANES), chunk.dtype),
        in_specs=[pl.BlockSpec(memory_space=pltpu.VMEM)] * 2,
        out_specs=pl.BlockSpec(memory_space=pltpu.VMEM),
        compiler_params=pltpu.CompilerParams(vmem_limit_bytes=4 << 20),
        cost_estimate=pl.CostEstimate(flops=1024, bytes_accessed=1024, transcendentals=0),
        name="attach",
    )(chunk, block)


def mark_kernel(*refs):
    refs[-1][...] = jnp.zeros(refs[-1].shape, refs[-1].dtype)


def mark(*after):
    return pl.pallas_call(
        mark_kernel,
        out_shape=jax.ShapeDtypeStruct((8, LANES), jnp.float32),
        in_specs=[pl.BlockSpec(memory_space=pl.ANY)] * len(after),
        out_specs=pl.BlockSpec(memory_space=pltpu.VMEM),
        compiler_params=pltpu.CompilerParams(vmem_limit_bytes=1 << 20),
        cost_estimate=pl.CostEstimate(flops=6*10**10, bytes_accessed=1024, transcendentals=0),
        name="mark",
    )(*after)


def resident(tokens, expert_ids, combine_weights, gate_weight, up_weight):
    experts = gate_weight.shape[0]
    owners = lax.axis_size("ep")
    tie = lax.optimization_barrier

    def swap(part):
        return lax.ppermute(part, "tp", [(0, 1), (1, 0)])

    def onward(right, left):
        return ring_send(right, owners, 1), ring_send(left, owners, -1)

    tiles = tuple(range(experts * 3 // 2))
    parts = tiles[:2], tiles[2:5], tiles[5:8], tiles[8:]
    packed, first, rest = begin(tokens, expert_ids, combine_weights, gate_weight, up_weight, *parts[:2])
    right1, left1 = onward(packed, packed)
    own, other = [first], [swap(first)]
    after = other[0]
    for following in parts[2:]:
        coded, rest = code_weights(gate_weight, up_weight, rest, following, after)
        own.append(coded)
        after = coded
    own += code_weights(gate_weight, up_weight, rest, (), after)
    other += [swap(part) for part in own[1:]]

    right1, left1, point = tie((right1, left1, mark(right1, left1, own[-1])))
    right2, left2 = onward(right1, left1)
    from1, back1 = hidden_units([right1, left1], own, other, experts, point)
    right3, left3 = onward(attach(right2, back1), attach(left2, from1))
    done = {-1: right3, 1: left3}
    from2, back2 = hidden_units([right2, left2], own, other, experts)
    done[2], done[-2] = ring_send(from2, owners, -2), ring_send(back2, owners, 2)

    right3, _ = tie((right3, from2))
    left3, _ = tie((left3, back2))
    right4 = ring_send(right3, owners, 1)
    from3, back3 = hidden_units([right3, left3], own, other, experts)
    done[3], done[-3] = ring_send(from3, owners, -3), ring_send(back3, owners, 3)

    right4, _, done[2], done[-2] = tie((right4, from3, done[2], done[-2]))
    (from4,) = hidden_units([right4], own, other, experts)
    done[4] = ring_send(from4, owners, 4)
    (done[0],) = hidden_units([packed], own, other, experts)
    places = tuple(sorted(done))
    return join_units([done[p] for p in places], places, done[0].shape[1])


def block_scale(largest):
    scale = jnp.full(largest.shape, 2.0 ** (-40), jnp.float32)
    for exponent_value in range(-39, 9):
        power = 2.0**exponent_value
        scale = jnp.where(largest >= power, jnp.float32(power), scale)
    return scale * 0.25


def code_blocks(weight):
    shaped = weight.reshape(weight.shape[:-1] + (weight.shape[-1] // 32, 32))
    magnitude = jnp.abs(shaped).astype(jnp.float32)
    scale = block_scale(jnp.max(magnitude, axis=-1))[..., None]
    total = jnp.zeros(magnitude.shape, jnp.float32)
    for bound_value, step_value in zip(THRESHOLDS, STEPS_UP):
        total = total + jnp.where(magnitude > bound_value * scale, step_value, 0.0)
    signed = jnp.where(shaped < 0, -total, total) * scale
    return signed.reshape(weight.shape).astype(jnp.bfloat16)


def activate(gate_value, up_value):
    gate_clamped = jnp.minimum(gate_value, LIMIT)
    up_clamped = jnp.clip(up_value, -LIMIT, LIMIT)
    return gate_clamped * jax.nn.sigmoid(1.702 * gate_clamped) * (up_clamped + 1.0)


def dispatched(tokens, expert_ids, combine_weights, gate_weight, up_weight):
    experts = gate_weight.shape[0]
    owners = lax.axis_size("ep")
    cores = lax.axis_size("tp")
    tok_rows = tokens.shape[0]
    top_count = expert_ids.shape[1]
    width = tokens.shape[1]
    slots = max(2, 2 * tok_rows * top_count // experts)
    gate_split, up_split = (
        lax.all_to_all(gate_weight, "tp", split_axis=1, concat_axis=2, tiled=True),
        lax.all_to_all(up_weight, "tp", split_axis=1, concat_axis=2, tiled=True),
    )
    gate_local, up_local = (
        lax.all_to_all(gate_split, "ep", split_axis=0, concat_axis=1, tiled=True),
        lax.all_to_all(up_split, "ep", split_axis=0, concat_axis=1, tiled=True),
    )
    gate_coded = code_blocks(gate_local[0])
    up_coded = code_blocks(up_local[0])
    chosen = expert_ids.reshape(-1)
    onehot = (chosen[:, None] == jnp.arange(experts, dtype=jnp.int32)[None, :]).astype(jnp.int32)
    before = jnp.cumsum(onehot, axis=0, dtype=jnp.int32) - onehot
    ranking = jnp.sum(before * onehot, axis=1, dtype=jnp.int32)
    target = chosen * slots + ranking
    repeated = jnp.repeat(tokens, top_count, axis=0)
    outgoing = jnp.zeros((experts * slots, width), jnp.bfloat16).at[target].set(repeated)
    received = lax.all_to_all(
        outgoing.reshape(experts, slots, width), "ep", split_axis=0, concat_axis=0, tiled=True
    )
    piece = lax.all_gather(received.reshape(owners * slots, width), "tp", axis=0, tiled=True)
    gate_value = jnp.einsum("rd,fd->rf", piece, gate_coded, preferred_element_type=jnp.float32)
    up_value = jnp.einsum("rd,fd->rf", piece, up_coded, preferred_element_type=jnp.float32)
    actives = activate(gate_value, up_value).astype(jnp.bfloat16)
    shaped_back = actives.reshape(cores, owners, slots, actives.shape[1])
    returned = lax.all_to_all(
        lax.all_to_all(shaped_back, "ep", split_axis=1, concat_axis=1, tiled=True),
        "tp",
        split_axis=0,
        concat_axis=3,
        tiled=True,
    )
    flat_back = returned.reshape(experts * slots, returned.shape[3])
    values = flat_back[target].reshape(tok_rows, top_count, flat_back.shape[1])
    mixed = jnp.einsum("tk,tkf->tf", combine_weights, values.astype(jnp.float32))
    hidden_total = mixed.shape[1]
    quarter = hidden_total // (owners * cores)
    mixed = (
        mixed.reshape(tok_rows, cores, owners, quarter)
        .transpose(0, 2, 1, 3)
        .reshape(tok_rows, hidden_total)
    )
    return mixed.astype(jnp.bfloat16)


def per_device(tokens, expert_ids, combine_weights, gate_weight, up_weight):
    experts, units, depth = gate_weight.shape
    owners, cores = lax.axis_size("ep"), lax.axis_size("tp")
    fits = owners == 8 and cores == 2 and experts <= 4 * expert_ids.shape[1] and experts % 8 == 0
    fits = fits and units == 3 * LANES // 2 and depth % 256 == 0 and tokens.shape[0] % 64 == 0
    plan = resident if fits else dispatched
    return plan(tokens, expert_ids, combine_weights, gate_weight, up_weight)


def solution(mesh):
    return jax.shard_map(
        per_device,
        mesh=mesh,
        in_specs=(
            P(("groups", "ep", "tp"), None),
            P(("groups", "ep", "tp"), None),
            P(("groups", "ep", "tp"), None),
            P(None, "ep", "tp"),
            P(None, "ep", "tp"),
        ),
        out_specs=P(("groups", "ep", "tp"), None),
        check_vma=False,
    )
```

```python
import functools

import jax
import jax.numpy as jnp
from jax import lax
from jax.experimental import pallas as pl
from jax.experimental.pallas import tpu as pltpu
from jax.sharding import PartitionSpec as P

THRESHOLDS = (0.25, 0.75, 1.25, 1.75, 2.5, 3.5, 5.0)
STEPS_UP = (0.5, 0.5, 0.5, 0.5, 1.0, 1.0, 2.0)
LIMIT = 7.0
LANES = 128
BLOCK = 32


def ring_place(owner, owners):
    return jnp.where(owner % 2 == 0, owner // 2, owners - 1 - owner // 2)


def ring_owner(place, owners):
    return jnp.where(place < owners // 2, 2 * place, 2 * (owners - 1 - place) + 1)


def ring_send(value, owners, steps):
    order = list(range(0, owners, 2)) + list(range(1, owners, 2))[::-1]
    pairs = [
        (2 * order[p] + core, 2 * order[(p + sign * steps) % owners] + core)
        for core, sign in ((0, 1), (1, -1))
        for p in range(owners)
    ]
    return lax.ppermute(value, ("ep", "tp"), pairs)


def code_columns(entries):
    depth, count = entries.shape
    blocks = entries.reshape(depth // BLOCK, BLOCK, count)
    largest = jnp.max(jnp.abs(blocks), axis=1, keepdims=True)
    largest = jnp.maximum(largest, 2.0**-40)
    lifted = largest * 2.0**23
    power = jnp.minimum((largest * 0.7 + lifted) - lifted, 2.0**8)
    lowered = blocks * (1.0 - 2.0**-12)
    top = power * 1.5
    lowered = jnp.minimum(jnp.maximum(lowered, -top), top)
    least = power * (0.25 * (1.0 + 2.0**-10))
    anchor = jnp.maximum(jnp.abs(lowered), least) * 2.0**22
    return ((lowered + anchor) - anchor).reshape(depth, count)


def tile_rows(tile, experts):
    if tile < experts:
        return [(tile, 0, LANES)]
    pair = 2 * (tile - experts)
    return [(pair, LANES, LANES // 2), (pair + 1, LANES, LANES // 2)]


def code_tile(rows_ref, out_ref, first):
    depth = rows_ref.shape[1]
    for low in range(0, depth, 256):
        turned = rows_ref[:, low : low + 256].T.astype(jnp.float32)
        out_ref[low : low + 256, pl.ds(first, 256)] = code_columns(turned).astype(jnp.bfloat16)


def fetch_rows(gate_ref, up_ref, tiles, target, arrived):
    experts = gate_ref.shape[0]
    groups = []
    for n, tile in enumerate(tiles):
        group, at = [], 0
        for ref in (gate_ref, up_ref):
            for expert, first, count in tile_rows(tile, experts):
                source = ref.at[expert, first : first + count]
                group.append(pltpu.make_async_copy(source, target.at[n, at : at + count], arrived.at[n, len(group)]))
                at += count
        groups.append(group)
    return groups


def code_kernel(*refs, following):
    if following:
        gate_ref, up_ref, rows_ref, _, out_ref, rest_ref, arrived = refs
        groups = fetch_rows(gate_ref, up_ref, following, rest_ref, arrived)
    else:
        (rows_ref, _, out_ref), groups = refs, []
    for group in groups:
        for copy in group:
            copy.start()

    @pl.loop(0, rows_ref.shape[0])
    def _(n):
        code_tile(rows_ref.at[n], out_ref, pl.multiple_of(n * 256, 256))

    for group in groups:
        for copy in group:
            copy.wait()


def code_weights(gate, up, rows, following, after):
    tiles, _, depth = rows.shape
    outs = [pltpu.VMEM((depth, 256 * tiles), jnp.bfloat16)]
    operands, scratch = [rows, after], []
    spaces = [pltpu.VMEM, pl.ANY]
    if following:
        outs.append(pltpu.VMEM((len(following), 2 * LANES, depth), jnp.bfloat16))
        operands = [pltpu.with_memory_space_constraint(x, pltpu.HBM) for x in (gate, up)] + operands
        spaces = [pl.ANY, pl.ANY] + spaces
        scratch = [pltpu.SemaphoreType.DMA((len(following), 4))]
    return pl.pallas_call(
        functools.partial(code_kernel, following=following),
        out_shape=outs,
        in_specs=[pl.BlockSpec(memory_space=space) for space in spaces],
        out_specs=[pl.BlockSpec(memory_space=pltpu.VMEM)] * len(outs),
        scratch_shapes=scratch,
        compiler_params=pltpu.CompilerParams(vmem_limit_bytes=12 << 20),
        cost_estimate=pl.CostEstimate(flops=1024, bytes_accessed=1024, transcendentals=0),
        name="code",
    )(*operands)


def begin_kernel(
    tokens_ref, ids_ref, weights_ref, gate_ref, up_ref, packed_ref, out_ref, rest_ref, ids, weights, held, near, fetched,
    *, tiles, following,
):
    experts = gate_ref.shape[0]
    rows, width = tokens_ref.shape
    routes = [
        pltpu.make_async_copy(ids_ref, ids, near.at[0]),
        pltpu.make_async_copy(weights_ref, weights, near.at[1]),
    ]
    moved = pltpu.make_async_copy(tokens_ref, packed_ref.at[:, :width], near.at[2])
    now = len(tiles)
    groups = fetch_rows(gate_ref, up_ref, tiles, held, fetched)
    later = fetch_rows(gate_ref, up_ref, following, rest_ref, fetched.at[now:])
    for copy in routes + [moved]:
        copy.start()
    for group in groups + later:
        for copy in group:
            copy.start()
    for copy in routes:
        copy.wait()
    number = lax.broadcasted_iota(jnp.int32, (experts, rows), 0)
    mix = jnp.zeros((experts, rows), jnp.float32)
    for choice in range(ids_ref.shape[0]):
        mix += jnp.where(ids[choice : choice + 1, :] == number, weights[choice : choice + 1, :], 0.0)
    high = mix.astype(jnp.bfloat16).astype(jnp.float32)
    middle = (mix - high).astype(jnp.bfloat16).astype(jnp.float32)
    low = mix - high - middle
    fill = jnp.zeros((LANES - 3 * experts, rows), jnp.float32)
    packed_ref[:, width:] = jnp.concatenate([high, middle, low, fill], axis=0).T.astype(jnp.bfloat16)
    for n, group in enumerate(groups):
        for copy in group:
            copy.wait()
        code_tile(held.at[n], out_ref, 256 * n)
    for group in later:
        for copy in group:
            copy.wait()
    moved.wait()


def begin(tokens, expert_ids, combine_weights, gate, up, tiles, following):
    depth = gate.shape[2]
    rows, width = tokens.shape
    choices = expert_ids.shape[1]
    operands = (tokens, expert_ids.T, combine_weights.T, gate, up)
    return pl.pallas_call(
        functools.partial(begin_kernel, tiles=tiles, following=following),
        out_shape=[
            pltpu.VMEM((rows, width + LANES), jnp.bfloat16),
            pltpu.VMEM((depth, 256 * len(tiles)), jnp.bfloat16),
            pltpu.VMEM((len(following), 2 * LANES, depth), jnp.bfloat16),
        ],
        in_specs=[pl.BlockSpec(memory_space=pl.ANY)] * 5,
        out_specs=[pl.BlockSpec(memory_space=pltpu.VMEM)] * 3,
        scratch_shapes=[
            pltpu.VMEM((choices, rows), jnp.int32),
            pltpu.VMEM((choices, rows), jnp.float32),
            pltpu.VMEM((len(tiles), 2 * LANES, depth), jnp.bfloat16),
            pltpu.SemaphoreType.DMA((3,)),
            pltpu.SemaphoreType.DMA((len(tiles) + len(following), 4)),
        ],
        compiler_params=pltpu.CompilerParams(vmem_limit_bytes=16 << 20),
        cost_estimate=pl.CostEstimate(flops=1024, bytes_accessed=1024, transcendentals=0),
        name="begin",
    )(*(pltpu.with_memory_space_constraint(x, pltpu.HBM) for x in operands))


def hidden_kernel(*refs, count, pieces, after, experts):
    chunks = refs[:count]
    own = refs[count : count + pieces]
    other = refs[count + pieces : count + 2 * pieces]
    *outs, tok = refs[count + 2 * pieces + after :]
    sizes = [chunk.shape[0] for chunk in chunks]
    width = tok.shape[1]
    core = lax.axis_index("tp")
    depth = own[0].shape[0]
    total = tok.shape[0]
    at = 0
    mixes = []
    for chunk, rows in zip(chunks, sizes):
        tok[at : at + rows, :] = chunk[:, :width]
        parts = chunk[:, width : width + LANES].astype(jnp.float32)
        mixes.append(parts[:, :experts] + parts[:, experts : 2 * experts] + parts[:, 2 * experts : 3 * experts])
        at += rows
    if at < total:
        tok[at:, :] = jnp.zeros((total - at, width), tok.dtype)
        mixes.append(jnp.zeros((total - at, experts), jnp.float32))
    mix = jnp.concatenate(mixes, axis=0) if len(mixes) > 1 else mixes[0]
    near = tok[:, pl.ds(pl.multiple_of(core * depth, LANES), depth)]
    far = tok[:, pl.ds(pl.multiple_of((1 - core) * depth, LANES), depth)]
    lane = lax.broadcasted_iota(jnp.int32, (total, LANES), 1)
    first_sum = jnp.zeros((total, LANES), jnp.float32)
    second_sum = jnp.zeros((total, LANES), jnp.float32)
    places = [(piece, at) for piece in range(pieces) for at in range(0, own[piece].shape[1], 256)]
    for tile, (piece, at) in enumerate(places):
        columns = slice(at, at + 256)
        both = jnp.dot(near, own[piece][:, columns], preferred_element_type=jnp.float32)
        both += jnp.dot(far, other[piece][:, columns], preferred_element_type=jnp.float32)
        gate = jnp.minimum(both[:, :LANES], LIMIT)
        up = jnp.clip(both[:, LANES:], -LIMIT, LIMIT)
        active = gate * jax.nn.sigmoid(1.702 * gate) * (up + 1.0)
        active = active.astype(jnp.bfloat16).astype(jnp.float32)
        if tile < experts:
            first_sum += active * mix[:, tile : tile + 1]
        else:
            pair = 2 * (tile - experts)
            second_sum += active * jnp.where(lane < LANES // 2, mix[:, pair : pair + 1], mix[:, pair + 1 : pair + 2])
    last = second_sum[:, : LANES // 2] + second_sum[:, LANES // 2 :]
    at = 0
    for out, rows in zip(outs, sizes):
        out[:, :LANES] = first_sum[at : at + rows].astype(jnp.bfloat16)
        out[:, LANES:] = last[at : at + rows].astype(jnp.bfloat16)
        at += rows


def hidden_units(chunks, own, other, experts, *after):
    units = 3 * LANES // 2
    sizes = [chunk.shape[0] for chunk in chunks]
    total, width = max(sum(sizes), LANES), 2 * own[0].shape[0]
    return pl.pallas_call(
        functools.partial(hidden_kernel, count=len(chunks), pieces=len(own), after=len(after), experts=experts),
        out_shape=[jax.ShapeDtypeStruct((rows, units), jnp.bfloat16) for rows in sizes],
        in_specs=[pl.BlockSpec(memory_space=pltpu.VMEM)] * (len(chunks) + 2 * len(own))
        + [pl.BlockSpec(memory_space=pl.ANY)] * len(after),
        out_specs=[pl.BlockSpec(memory_space=pltpu.VMEM)] * len(chunks),
        scratch_shapes=[pltpu.VMEM((total, width), jnp.bfloat16)],
        compiler_params=pltpu.CompilerParams(vmem_limit_bytes=20 << 20),
        cost_estimate=pl.CostEstimate(flops=12*10**9, bytes_accessed=1024, transcendentals=0),
        name="hidden",
    )(*chunks, *own, *other, *after)


def join_kernel(*refs, steps):
    blocks, out_ref, held = refs[: len(steps)], refs[len(steps)], refs[len(steps) + 1]
    owners = lax.axis_size("ep")
    place = ring_place(lax.axis_index("ep"), owners)
    sign = 1 - 2 * lax.axis_index("tp")
    units = held.shape[2]
    for block, step in zip(blocks, steps):
        source = ring_owner((place + sign * step + owners) % owners, owners)
        width = block.shape[1]
        if width == units:
            held[source] = block[...]
        else:
            held[source, :, :LANES] = block[:, width - LANES :]
            held[source, :, LANES:] = block[:, width - LANES - LANES // 2 : width - LANES]
    for owner in range(owners):
        out_ref[:, owner * units : (owner + 1) * units] = held[owner]


def join_units(blocks, steps, units):
    rows = blocks[0].shape[0]
    return pl.pallas_call(
        functools.partial(join_kernel, steps=steps),
        out_shape=jax.ShapeDtypeStruct((rows, units * len(steps)), jnp.bfloat16),
        in_specs=[pl.BlockSpec(memory_space=pltpu.VMEM)] * len(blocks),
        out_specs=pl.BlockSpec(memory_space=pltpu.VMEM),
        scratch_shapes=[pltpu.VMEM((len(steps), rows, units), jnp.bfloat16)],
        compiler_params=pltpu.CompilerParams(vmem_limit_bytes=4 << 20),
        name="join",
    )(*blocks)


def attach_kernel(chunk_ref, block_ref, out_ref):
    width = chunk_ref.shape[1]
    out_ref[:, : width - LANES] = chunk_ref[:, : width - LANES]
    beside = [chunk_ref[:, width - LANES : width - LANES // 2], block_ref[:, LANES:]]
    out_ref[:, width - LANES : width] = jnp.concatenate(beside, axis=1)
    out_ref[:, width:] = block_ref[:, :LANES]


def attach(chunk, block):
    rows, width = chunk.shape
    return pl.pallas_call(
        attach_kernel,
        out_shape=jax.ShapeDtypeStruct((rows, width + LANES), chunk.dtype),
        in_specs=[pl.BlockSpec(memory_space=pltpu.VMEM)] * 2,
        out_specs=pl.BlockSpec(memory_space=pltpu.VMEM),
        compiler_params=pltpu.CompilerParams(vmem_limit_bytes=4 << 20),
        cost_estimate=pl.CostEstimate(flops=1024, bytes_accessed=1024, transcendentals=0),
        name="attach",
    )(chunk, block)


def mark_kernel(*refs):
    refs[-1][...] = jnp.zeros(refs[-1].shape, refs[-1].dtype)


def mark(*after):
    return pl.pallas_call(
        mark_kernel,
        out_shape=jax.ShapeDtypeStruct((8, LANES), jnp.float32),
        in_specs=[pl.BlockSpec(memory_space=pl.ANY)] * len(after),
        out_specs=pl.BlockSpec(memory_space=pltpu.VMEM),
        compiler_params=pltpu.CompilerParams(vmem_limit_bytes=1 << 20),
        cost_estimate=pl.CostEstimate(flops=6*10**10, bytes_accessed=1024, transcendentals=0),
        name="mark",
    )(*after)


def resident(tokens, expert_ids, combine_weights, gate_weight, up_weight):
    experts = gate_weight.shape[0]
    owners = lax.axis_size("ep")
    tie = lax.optimization_barrier

    def swap(part):
        return lax.ppermute(part, "tp", [(0, 1), (1, 0)])

    def onward(right, left):
        return ring_send(right, owners, 1), ring_send(left, owners, -1)

    tiles = tuple(range(experts * 3 // 2))
    parts = tiles[:1], tiles[1:6], tiles[6:]
    packed, first, rest = begin(tokens, expert_ids, combine_weights, gate_weight, up_weight, *parts[:2])
    right1, left1 = onward(packed, packed)
    own, other = [first], [swap(first)]
    after = other[0]
    for following in parts[2:]:
        coded, rest = code_weights(gate_weight, up_weight, rest, following, after)
        own.append(coded)
        after = coded
    own += code_weights(gate_weight, up_weight, rest, (), after)
    other += [swap(part) for part in own[1:]]

    right1, left1, point = tie((right1, left1, mark(right1, left1, own[-1])))
    right2, left2 = onward(right1, left1)
    from1, back1 = hidden_units([right1, left1], own, other, experts, point)
    right3, left3 = onward(attach(right2, back1), attach(left2, from1))
    done = {-1: right3, 1: left3}
    from2, back2 = hidden_units([right2, left2], own, other, experts)
    done[2], done[-2] = ring_send(from2, owners, -2), ring_send(back2, owners, 2)

    right3, _ = tie((right3, from2))
    left3, _ = tie((left3, back2))
    right4 = ring_send(right3, owners, 1)
    from3, back3 = hidden_units([right3, left3], own, other, experts)
    done[3], done[-3] = ring_send(from3, owners, -3), ring_send(back3, owners, 3)

    right4, _, done[2], done[-2] = tie((right4, from3, done[2], done[-2]))
    (from4,) = hidden_units([right4], own, other, experts)
    done[4] = ring_send(from4, owners, 4)
    (done[0],) = hidden_units([packed], own, other, experts)
    places = tuple(sorted(done))
    return join_units([done[p] for p in places], places, done[0].shape[1])


def block_scale(largest):
    scale = jnp.full(largest.shape, 2.0 ** (-40), jnp.float32)
    for exponent_value in range(-39, 9):
        power = 2.0**exponent_value
        scale = jnp.where(largest >= power, jnp.float32(power), scale)
    return scale * 0.25


def code_blocks(weight):
    shaped = weight.reshape(weight.shape[:-1] + (weight.shape[-1] // 32, 32))
    magnitude = jnp.abs(shaped).astype(jnp.float32)
    scale = block_scale(jnp.max(magnitude, axis=-1))[..., None]
    total = jnp.zeros(magnitude.shape, jnp.float32)
    for bound_value, step_value in zip(THRESHOLDS, STEPS_UP):
        total = total + jnp.where(magnitude > bound_value * scale, step_value, 0.0)
    signed = jnp.where(shaped < 0, -total, total) * scale
    return signed.reshape(weight.shape).astype(jnp.bfloat16)


def activate(gate_value, up_value):
    gate_clamped = jnp.minimum(gate_value, LIMIT)
    up_clamped = jnp.clip(up_value, -LIMIT, LIMIT)
    return gate_clamped * jax.nn.sigmoid(1.702 * gate_clamped) * (up_clamped + 1.0)


def dispatched(tokens, expert_ids, combine_weights, gate_weight, up_weight):
    experts = gate_weight.shape[0]
    owners = lax.axis_size("ep")
    cores = lax.axis_size("tp")
    tok_rows = tokens.shape[0]
    top_count = expert_ids.shape[1]
    width = tokens.shape[1]
    slots = max(2, 2 * tok_rows * top_count // experts)
    gate_split, up_split = (
        lax.all_to_all(gate_weight, "tp", split_axis=1, concat_axis=2, tiled=True),
        lax.all_to_all(up_weight, "tp", split_axis=1, concat_axis=2, tiled=True),
    )
    gate_local, up_local = (
        lax.all_to_all(gate_split, "ep", split_axis=0, concat_axis=1, tiled=True),
        lax.all_to_all(up_split, "ep", split_axis=0, concat_axis=1, tiled=True),
    )
    gate_coded = code_blocks(gate_local[0])
    up_coded = code_blocks(up_local[0])
    chosen = expert_ids.reshape(-1)
    onehot = (chosen[:, None] == jnp.arange(experts, dtype=jnp.int32)[None, :]).astype(jnp.int32)
    before = jnp.cumsum(onehot, axis=0, dtype=jnp.int32) - onehot
    ranking = jnp.sum(before * onehot, axis=1, dtype=jnp.int32)
    target = chosen * slots + ranking
    repeated = jnp.repeat(tokens, top_count, axis=0)
    outgoing = jnp.zeros((experts * slots, width), jnp.bfloat16).at[target].set(repeated)
    received = lax.all_to_all(
        outgoing.reshape(experts, slots, width), "ep", split_axis=0, concat_axis=0, tiled=True
    )
    piece = lax.all_gather(received.reshape(owners * slots, width), "tp", axis=0, tiled=True)
    gate_value = jnp.einsum("rd,fd->rf", piece, gate_coded, preferred_element_type=jnp.float32)
    up_value = jnp.einsum("rd,fd->rf", piece, up_coded, preferred_element_type=jnp.float32)
    actives = activate(gate_value, up_value).astype(jnp.bfloat16)
    shaped_back = actives.reshape(cores, owners, slots, actives.shape[1])
    returned = lax.all_to_all(
        lax.all_to_all(shaped_back, "ep", split_axis=1, concat_axis=1, tiled=True),
        "tp",
        split_axis=0,
        concat_axis=3,
        tiled=True,
    )
    flat_back = returned.reshape(experts * slots, returned.shape[3])
    values = flat_back[target].reshape(tok_rows, top_count, flat_back.shape[1])
    mixed = jnp.einsum("tk,tkf->tf", combine_weights, values.astype(jnp.float32))
    hidden_total = mixed.shape[1]
    quarter = hidden_total // (owners * cores)
    mixed = (
        mixed.reshape(tok_rows, cores, owners, quarter)
        .transpose(0, 2, 1, 3)
        .reshape(tok_rows, hidden_total)
    )
    return mixed.astype(jnp.bfloat16)


def per_device(tokens, expert_ids, combine_weights, gate_weight, up_weight):
    experts, units, depth = gate_weight.shape
    owners, cores = lax.axis_size("ep"), lax.axis_size("tp")
    fits = owners == 8 and cores == 2 and experts <= 4 * expert_ids.shape[1] and experts % 8 == 0
    fits = fits and units == 3 * LANES // 2 and depth % 256 == 0 and tokens.shape[0] % 64 == 0
    plan = resident if fits else dispatched
    return plan(tokens, expert_ids, combine_weights, gate_weight, up_weight)


def solution(mesh):
    return jax.shard_map(
        per_device,
        mesh=mesh,
        in_specs=(
            P(("groups", "ep", "tp"), None),
            P(("groups", "ep", "tp"), None),
            P(("groups", "ep", "tp"), None),
            P(None, "ep", "tp"),
            P(None, "ep", "tp"),
        ),
        out_specs=P(("groups", "ep", "tp"), None),
        check_vma=False,
    )
```

```python
import functools

import jax
import jax.numpy as jnp
from jax import lax
from jax.experimental import pallas as pl
from jax.experimental.pallas import tpu as pltpu
from jax.sharding import PartitionSpec as P

THRESHOLDS = (0.25, 0.75, 1.25, 1.75, 2.5, 3.5, 5.0)
STEPS_UP = (0.5, 0.5, 0.5, 0.5, 1.0, 1.0, 2.0)
LIMIT = 7.0
LANES = 128
BLOCK = 32


def ring_place(owner, owners):
    return jnp.where(owner % 2 == 0, owner // 2, owners - 1 - owner // 2)


def ring_owner(place, owners):
    return jnp.where(place < owners // 2, 2 * place, 2 * (owners - 1 - place) + 1)


def ring_send(value, owners, steps):
    order = list(range(0, owners, 2)) + list(range(1, owners, 2))[::-1]
    return lax.ppermute(value, "ep", [(order[p], order[(p + steps) % owners]) for p in range(owners)])


def code_columns(entries):
    depth, count = entries.shape
    blocks = entries.reshape(depth // BLOCK, BLOCK, count)
    largest = jnp.max(jnp.abs(blocks), axis=1, keepdims=True)
    largest = jnp.maximum(largest, 2.0**-40)
    lifted = largest * 2.0**23
    power = jnp.minimum((largest * 0.7 + lifted) - lifted, 2.0**8)
    lowered = blocks * (1.0 - 2.0**-12)
    top = power * 1.5
    lowered = jnp.minimum(jnp.maximum(lowered, -top), top)
    least = power * (0.25 * (1.0 + 2.0**-10))
    anchor = jnp.maximum(jnp.abs(lowered), least) * 2.0**22
    return ((lowered + anchor) - anchor).reshape(depth, count)


def tile_rows(tile, experts):
    if tile < experts:
        return [(tile, 0, LANES)]
    pair = 2 * (tile - experts)
    return [(pair, LANES, LANES // 2), (pair + 1, LANES, LANES // 2)]


def code_tile(rows_ref, out_ref, first):
    depth = rows_ref.shape[1]
    for low in range(0, depth, 256):
        turned = rows_ref[:, low : low + 256].T.astype(jnp.float32)
        out_ref[low : low + 256, pl.ds(first, 256)] = code_columns(turned).astype(jnp.bfloat16)


def fetch_rows(gate_ref, up_ref, tiles, target, arrived):
    experts = gate_ref.shape[0]
    groups = []
    for n, tile in enumerate(tiles):
        group, at = [], 0
        for ref in (gate_ref, up_ref):
            for expert, first, count in tile_rows(tile, experts):
                source = ref.at[expert, first : first + count]
                group.append(pltpu.make_async_copy(source, target.at[n, at : at + count], arrived.at[n, len(group)]))
                at += count
        groups.append(group)
    return groups


def code_kernel(*refs, following):
    if following:
        gate_ref, up_ref, rows_ref, _, out_ref, rest_ref, arrived = refs
        groups = fetch_rows(gate_ref, up_ref, following, rest_ref, arrived)
    else:
        (rows_ref, _, out_ref), groups = refs, []
    for group in groups:
        for copy in group:
            copy.start()

    @pl.loop(0, rows_ref.shape[0])
    def _(n):
        code_tile(rows_ref.at[n], out_ref, pl.multiple_of(n * 256, 256))

    for group in groups:
        for copy in group:
            copy.wait()


def code_weights(gate, up, rows, following, after):
    tiles, _, depth = rows.shape
    outs = [pltpu.VMEM((depth, 256 * tiles), jnp.bfloat16)]
    operands, scratch = [rows, after], []
    spaces = [pltpu.VMEM, pl.ANY]
    if following:
        outs.append(pltpu.VMEM((len(following), 2 * LANES, depth), jnp.bfloat16))
        operands = [pltpu.with_memory_space_constraint(x, pltpu.HBM) for x in (gate, up)] + operands
        spaces = [pl.ANY, pl.ANY] + spaces
        scratch = [pltpu.SemaphoreType.DMA((len(following), 4))]
    return pl.pallas_call(
        functools.partial(code_kernel, following=following),
        out_shape=outs,
        in_specs=[pl.BlockSpec(memory_space=space) for space in spaces],
        out_specs=[pl.BlockSpec(memory_space=pltpu.VMEM)] * len(outs),
        scratch_shapes=scratch,
        compiler_params=pltpu.CompilerParams(vmem_limit_bytes=12 << 20),
        cost_estimate=pl.CostEstimate(flops=1024, bytes_accessed=1024, transcendentals=0),
        name="code",
    )(*operands)


def begin_kernel(
    tokens_ref, ids_ref, weights_ref, gate_ref, up_ref, packed_ref, out_ref, rest_ref, ids, weights, held, near, fetched,
    *, tiles, following,
):
    experts = gate_ref.shape[0]
    rows, width = tokens_ref.shape
    routes = [
        pltpu.make_async_copy(ids_ref, ids, near.at[0]),
        pltpu.make_async_copy(weights_ref, weights, near.at[1]),
    ]
    moved = pltpu.make_async_copy(tokens_ref, packed_ref.at[:, :width], near.at[2])
    now = len(tiles)
    groups = fetch_rows(gate_ref, up_ref, tiles, held, fetched)
    later = fetch_rows(gate_ref, up_ref, following, rest_ref, fetched.at[now:])
    for copy in routes + [moved]:
        copy.start()
    for group in groups + later:
        for copy in group:
            copy.start()
    for copy in routes:
        copy.wait()
    number = lax.broadcasted_iota(jnp.int32, (experts, rows), 0)
    mix = jnp.zeros((experts, rows), jnp.float32)
    for choice in range(ids_ref.shape[0]):
        mix += jnp.where(ids[choice : choice + 1, :] == number, weights[choice : choice + 1, :], 0.0)
    high = mix.astype(jnp.bfloat16).astype(jnp.float32)
    middle = (mix - high).astype(jnp.bfloat16).astype(jnp.float32)
    low = mix - high - middle
    fill = jnp.zeros((LANES - 3 * experts, rows), jnp.float32)
    packed_ref[:, width:] = jnp.concatenate([high, middle, low, fill], axis=0).T.astype(jnp.bfloat16)
    for n, group in enumerate(groups):
        for copy in group:
            copy.wait()
        code_tile(held.at[n], out_ref, 256 * n)
    for group in later:
        for copy in group:
            copy.wait()
    moved.wait()


def begin(tokens, expert_ids, combine_weights, gate, up, tiles, following):
    depth = gate.shape[2]
    rows, width = tokens.shape
    choices = expert_ids.shape[1]
    operands = (tokens, expert_ids.T, combine_weights.T, gate, up)
    return pl.pallas_call(
        functools.partial(begin_kernel, tiles=tiles, following=following),
        out_shape=[
            pltpu.VMEM((rows, width + LANES), jnp.bfloat16),
            pltpu.VMEM((depth, 256 * len(tiles)), jnp.bfloat16),
            pltpu.VMEM((len(following), 2 * LANES, depth), jnp.bfloat16),
        ],
        in_specs=[pl.BlockSpec(memory_space=pl.ANY)] * 5,
        out_specs=[pl.BlockSpec(memory_space=pltpu.VMEM)] * 3,
        scratch_shapes=[
            pltpu.VMEM((choices, rows), jnp.int32),
            pltpu.VMEM((choices, rows), jnp.float32),
            pltpu.VMEM((len(tiles), 2 * LANES, depth), jnp.bfloat16),
            pltpu.SemaphoreType.DMA((3,)),
            pltpu.SemaphoreType.DMA((len(tiles) + len(following), 4)),
        ],
        compiler_params=pltpu.CompilerParams(vmem_limit_bytes=16 << 20),
        cost_estimate=pl.CostEstimate(flops=1024, bytes_accessed=1024, transcendentals=0),
        name="begin",
    )(*(pltpu.with_memory_space_constraint(x, pltpu.HBM) for x in operands))


def hidden_kernel(*refs, count, pieces, after, experts):
    chunks = refs[:count]
    own = refs[count : count + pieces]
    other = refs[count + pieces : count + 2 * pieces]
    *outs, tok = refs[count + 2 * pieces + after :]
    sizes = [chunk.shape[0] for chunk in chunks]
    width = tok.shape[1]
    core = lax.axis_index("tp")
    depth = own[0].shape[0]
    total = tok.shape[0]
    at = 0
    mixes = []
    for chunk, rows in zip(chunks, sizes):
        tok[at : at + rows, :] = chunk[:, :width]
        parts = chunk[:, width : width + LANES].astype(jnp.float32)
        mixes.append(parts[:, :experts] + parts[:, experts : 2 * experts] + parts[:, 2 * experts : 3 * experts])
        at += rows
    if at < total:
        tok[at:, :] = jnp.zeros((total - at, width), tok.dtype)
        mixes.append(jnp.zeros((total - at, experts), jnp.float32))
    mix = jnp.concatenate(mixes, axis=0) if len(mixes) > 1 else mixes[0]
    near = tok[:, pl.ds(pl.multiple_of(core * depth, LANES), depth)]
    far = tok[:, pl.ds(pl.multiple_of((1 - core) * depth, LANES), depth)]
    lane = lax.broadcasted_iota(jnp.int32, (total, LANES), 1)
    first_sum = jnp.zeros((total, LANES), jnp.float32)
    second_sum = jnp.zeros((total, LANES), jnp.float32)
    places = [(piece, at) for piece in range(pieces) for at in range(0, own[piece].shape[1], 256)]
    for tile, (piece, at) in enumerate(places):
        columns = slice(at, at + 256)
        both = jnp.dot(near, own[piece][:, columns], preferred_element_type=jnp.float32)
        both += jnp.dot(far, other[piece][:, columns], preferred_element_type=jnp.float32)
        gate = jnp.minimum(both[:, :LANES], LIMIT)
        up = jnp.clip(both[:, LANES:], -LIMIT, LIMIT)
        active = gate * jax.nn.sigmoid(1.702 * gate) * (up + 1.0)
        active = active.astype(jnp.bfloat16).astype(jnp.float32)
        if tile < experts:
            first_sum += active * mix[:, tile : tile + 1]
        else:
            pair = 2 * (tile - experts)
            second_sum += active * jnp.where(lane < LANES // 2, mix[:, pair : pair + 1], mix[:, pair + 1 : pair + 2])
    last = second_sum[:, : LANES // 2] + second_sum[:, LANES // 2 :]
    at = 0
    for out, rows in zip(outs, sizes):
        out[:, :LANES] = first_sum[at : at + rows].astype(jnp.bfloat16)
        out[:, LANES:] = last[at : at + rows].astype(jnp.bfloat16)
        at += rows


def hidden_units(chunks, own, other, experts, *after):
    units = 3 * LANES // 2
    sizes = [chunk.shape[0] for chunk in chunks]
    total, width = max(sum(sizes), LANES), 2 * own[0].shape[0]
    return pl.pallas_call(
        functools.partial(hidden_kernel, count=len(chunks), pieces=len(own), after=len(after), experts=experts),
        out_shape=[jax.ShapeDtypeStruct((rows, units), jnp.bfloat16) for rows in sizes],
        in_specs=[pl.BlockSpec(memory_space=pltpu.VMEM)] * (len(chunks) + 2 * len(own))
        + [pl.BlockSpec(memory_space=pl.ANY)] * len(after),
        out_specs=[pl.BlockSpec(memory_space=pltpu.VMEM)] * len(chunks),
        scratch_shapes=[pltpu.VMEM((total, width), jnp.bfloat16)],
        compiler_params=pltpu.CompilerParams(vmem_limit_bytes=20 << 20),
        cost_estimate=pl.CostEstimate(flops=12*10**9, bytes_accessed=1024, transcendentals=0),
        name="hidden",
    )(*chunks, *own, *other, *after)


def join_kernel(*refs, steps):
    blocks, out_ref, held = refs[: len(steps)], refs[len(steps)], refs[len(steps) + 1]
    owners = lax.axis_size("ep")
    place = ring_place(lax.axis_index("ep"), owners)
    units = held.shape[2]
    for block, step in zip(blocks, steps):
        source = ring_owner((place + step + owners) % owners, owners)
        width = block.shape[1]
        if width == units:
            held[source] = block[...]
        else:
            held[source, :, :LANES] = block[:, width - LANES :]
            held[source, :, LANES:] = block[:, width - LANES - LANES // 2 : width - LANES]
    for owner in range(owners):
        out_ref[:, owner * units : (owner + 1) * units] = held[owner]


def join_units(blocks, steps, units):
    rows = blocks[0].shape[0]
    return pl.pallas_call(
        functools.partial(join_kernel, steps=steps),
        out_shape=jax.ShapeDtypeStruct((rows, units * len(steps)), jnp.bfloat16),
        in_specs=[pl.BlockSpec(memory_space=pltpu.VMEM)] * len(blocks),
        out_specs=pl.BlockSpec(memory_space=pltpu.VMEM),
        scratch_shapes=[pltpu.VMEM((len(steps), rows, units), jnp.bfloat16)],
        compiler_params=pltpu.CompilerParams(vmem_limit_bytes=4 << 20),
        name="join",
    )(*blocks)


def attach_kernel(chunk_ref, block_ref, out_ref):
    width = chunk_ref.shape[1]
    out_ref[:, : width - LANES] = chunk_ref[:, : width - LANES]
    beside = [chunk_ref[:, width - LANES : width - LANES // 2], block_ref[:, LANES:]]
    out_ref[:, width - LANES : width] = jnp.concatenate(beside, axis=1)
    out_ref[:, width:] = block_ref[:, :LANES]


def attach(chunk, block):
    rows, width = chunk.shape
    return pl.pallas_call(
        attach_kernel,
        out_shape=jax.ShapeDtypeStruct((rows, width + LANES), chunk.dtype),
        in_specs=[pl.BlockSpec(memory_space=pltpu.VMEM)] * 2,
        out_specs=pl.BlockSpec(memory_space=pltpu.VMEM),
        compiler_params=pltpu.CompilerParams(vmem_limit_bytes=4 << 20),
        cost_estimate=pl.CostEstimate(flops=1024, bytes_accessed=1024, transcendentals=0),
        name="attach",
    )(chunk, block)


def mark_kernel(*refs):
    refs[-1][...] = jnp.zeros(refs[-1].shape, refs[-1].dtype)


def mark(*after):
    return pl.pallas_call(
        mark_kernel,
        out_shape=jax.ShapeDtypeStruct((8, LANES), jnp.float32),
        in_specs=[pl.BlockSpec(memory_space=pl.ANY)] * len(after),
        out_specs=pl.BlockSpec(memory_space=pltpu.VMEM),
        compiler_params=pltpu.CompilerParams(vmem_limit_bytes=1 << 20),
        cost_estimate=pl.CostEstimate(flops=6*10**10, bytes_accessed=1024, transcendentals=0),
        name="mark",
    )(*after)


def resident(tokens, expert_ids, combine_weights, gate_weight, up_weight):
    experts = gate_weight.shape[0]
    owners = lax.axis_size("ep")
    tie = lax.optimization_barrier

    def swap(part):
        return lax.ppermute(part, "tp", [(0, 1), (1, 0)])

    def onward(right, left):
        return ring_send(right, owners, 1), ring_send(left, owners, -1)

    tiles = tuple(range(experts * 3 // 2))
    parts = tiles[:1], tiles[1:6], tiles[6:]
    packed, first, rest = begin(tokens, expert_ids, combine_weights, gate_weight, up_weight, *parts[:2])
    right1, left1 = onward(packed, packed)
    own, other = [first], [swap(first)]
    after = other[0]
    for following in parts[2:]:
        coded, rest = code_weights(gate_weight, up_weight, rest, following, after)
        own.append(coded)
        after = coded
    own += code_weights(gate_weight, up_weight, rest, (), after)
    other += [swap(part) for part in own[1:]]

    right1, left1, point = tie((right1, left1, mark(right1, left1, own[-1])))
    right2, left2 = onward(right1, left1)
    from1, back1 = hidden_units([right1, left1], own, other, experts, point)
    right3, left3 = onward(attach(right2, back1), attach(left2, from1))
    done = {-1: right3, 1: left3}
    from2, back2 = hidden_units([right2, left2], own, other, experts)
    done[2], done[-2] = ring_send(from2, owners, -2), ring_send(back2, owners, 2)

    right3, _ = tie((right3, from2))
    left3, _ = tie((left3, back2))
    right4 = ring_send(right3, owners, 1)
    from3, back3 = hidden_units([right3, left3], own, other, experts)
    done[3], done[-3] = ring_send(from3, owners, -3), ring_send(back3, owners, 3)

    right4, _, done[2], done[-2] = tie((right4, from3, done[2], done[-2]))
    (from4,) = hidden_units([right4], own, other, experts)
    done[4] = ring_send(from4, owners, 4)
    (done[0],) = hidden_units([packed], own, other, experts)
    places = tuple(sorted(done))
    return join_units([done[p] for p in places], places, done[0].shape[1])


def block_scale(largest):
    scale = jnp.full(largest.shape, 2.0 ** (-40), jnp.float32)
    for exponent_value in range(-39, 9):
        power = 2.0**exponent_value
        scale = jnp.where(largest >= power, jnp.float32(power), scale)
    return scale * 0.25


def code_blocks(weight):
    shaped = weight.reshape(weight.shape[:-1] + (weight.shape[-1] // 32, 32))
    magnitude = jnp.abs(shaped).astype(jnp.float32)
    scale = block_scale(jnp.max(magnitude, axis=-1))[..., None]
    total = jnp.zeros(magnitude.shape, jnp.float32)
    for bound_value, step_value in zip(THRESHOLDS, STEPS_UP):
        total = total + jnp.where(magnitude > bound_value * scale, step_value, 0.0)
    signed = jnp.where(shaped < 0, -total, total) * scale
    return signed.reshape(weight.shape).astype(jnp.bfloat16)


def activate(gate_value, up_value):
    gate_clamped = jnp.minimum(gate_value, LIMIT)
    up_clamped = jnp.clip(up_value, -LIMIT, LIMIT)
    return gate_clamped * jax.nn.sigmoid(1.702 * gate_clamped) * (up_clamped + 1.0)


def dispatched(tokens, expert_ids, combine_weights, gate_weight, up_weight):
    experts = gate_weight.shape[0]
    owners = lax.axis_size("ep")
    cores = lax.axis_size("tp")
    tok_rows = tokens.shape[0]
    top_count = expert_ids.shape[1]
    width = tokens.shape[1]
    slots = max(2, 2 * tok_rows * top_count // experts)
    gate_split, up_split = (
        lax.all_to_all(gate_weight, "tp", split_axis=1, concat_axis=2, tiled=True),
        lax.all_to_all(up_weight, "tp", split_axis=1, concat_axis=2, tiled=True),
    )
    gate_local, up_local = (
        lax.all_to_all(gate_split, "ep", split_axis=0, concat_axis=1, tiled=True),
        lax.all_to_all(up_split, "ep", split_axis=0, concat_axis=1, tiled=True),
    )
    gate_coded = code_blocks(gate_local[0])
    up_coded = code_blocks(up_local[0])
    chosen = expert_ids.reshape(-1)
    onehot = (chosen[:, None] == jnp.arange(experts, dtype=jnp.int32)[None, :]).astype(jnp.int32)
    before = jnp.cumsum(onehot, axis=0, dtype=jnp.int32) - onehot
    ranking = jnp.sum(before * onehot, axis=1, dtype=jnp.int32)
    target = chosen * slots + ranking
    repeated = jnp.repeat(tokens, top_count, axis=0)
    outgoing = jnp.zeros((experts * slots, width), jnp.bfloat16).at[target].set(repeated)
    received = lax.all_to_all(
        outgoing.reshape(experts, slots, width), "ep", split_axis=0, concat_axis=0, tiled=True
    )
    piece = lax.all_gather(received.reshape(owners * slots, width), "tp", axis=0, tiled=True)
    gate_value = jnp.einsum("rd,fd->rf", piece, gate_coded, preferred_element_type=jnp.float32)
    up_value = jnp.einsum("rd,fd->rf", piece, up_coded, preferred_element_type=jnp.float32)
    actives = activate(gate_value, up_value).astype(jnp.bfloat16)
    shaped_back = actives.reshape(cores, owners, slots, actives.shape[1])
    returned = lax.all_to_all(
        lax.all_to_all(shaped_back, "ep", split_axis=1, concat_axis=1, tiled=True),
        "tp",
        split_axis=0,
        concat_axis=3,
        tiled=True,
    )
    flat_back = returned.reshape(experts * slots, returned.shape[3])
    values = flat_back[target].reshape(tok_rows, top_count, flat_back.shape[1])
    mixed = jnp.einsum("tk,tkf->tf", combine_weights, values.astype(jnp.float32))
    hidden_total = mixed.shape[1]
    quarter = hidden_total // (owners * cores)
    mixed = (
        mixed.reshape(tok_rows, cores, owners, quarter)
        .transpose(0, 2, 1, 3)
        .reshape(tok_rows, hidden_total)
    )
    return mixed.astype(jnp.bfloat16)


def per_device(tokens, expert_ids, combine_weights, gate_weight, up_weight):
    experts, units, depth = gate_weight.shape
    owners, cores = lax.axis_size("ep"), lax.axis_size("tp")
    fits = owners == 8 and cores == 2 and experts <= 4 * expert_ids.shape[1] and experts % 8 == 0
    fits = fits and units == 3 * LANES // 2 and depth % 256 == 0 and tokens.shape[0] % 64 == 0
    plan = resident if fits else dispatched
    return plan(tokens, expert_ids, combine_weights, gate_weight, up_weight)


def solution(mesh):
    return jax.shard_map(
        per_device,
        mesh=mesh,
        in_specs=(
            P(("groups", "ep", "tp"), None),
            P(("groups", "ep", "tp"), None),
            P(("groups", "ep", "tp"), None),
            P(None, "ep", "tp"),
            P(None, "ep", "tp"),
        ),
        out_specs=P(("groups", "ep", "tp"), None),
        check_vma=False,
    )
```

```python
import functools

import jax
import jax.numpy as jnp
from jax import lax
from jax.experimental import pallas as pl
from jax.experimental.pallas import tpu as pltpu
from jax.sharding import PartitionSpec as P

THRESHOLDS = (0.25, 0.75, 1.25, 1.75, 2.5, 3.5, 5.0)
STEPS_UP = (0.5, 0.5, 0.5, 0.5, 1.0, 1.0, 2.0)
LIMIT = 7.0
LANES = 128
BLOCK = 32


def ring_place(owner, owners):
    return jnp.where(owner % 2 == 0, owner // 2, owners - 1 - owner // 2)


def ring_owner(place, owners):
    return jnp.where(place < owners // 2, 2 * place, 2 * (owners - 1 - place) + 1)


def ring_send(value, owners, steps):
    order = list(range(0, owners, 2)) + list(range(1, owners, 2))[::-1]
    return lax.ppermute(value, "ep", [(order[p], order[(p + steps) % owners]) for p in range(owners)])


def code_columns(entries):
    depth, count = entries.shape
    blocks = entries.reshape(depth // BLOCK, BLOCK, count)
    sizes = jnp.abs(blocks)
    sizes = jnp.maximum(sizes[:, : BLOCK // 2], sizes[:, BLOCK // 2 :]).astype(jnp.float32)
    largest = jnp.maximum(jnp.max(sizes, axis=1, keepdims=True), 2.0**-40)
    lifted = largest * 2.0**23
    power = jnp.minimum((largest * 0.7 + lifted) - lifted, 2.0**8)
    top = (power * 1.5).astype(jnp.bfloat16)
    blocks = jnp.minimum(jnp.maximum(blocks, -top), top)
    lowered = blocks.astype(jnp.float32) * (1.0 - 2.0**-12)
    least = power * (0.25 * (1.0 + 2.0**-10))
    anchor = jnp.maximum(jnp.abs(lowered), least) * 2.0**22
    return ((lowered + anchor) - anchor).reshape(depth, count).astype(jnp.bfloat16)


def tile_rows(tile, experts):
    if tile < experts:
        return [(tile, 0, LANES)]
    pair = 2 * (tile - experts)
    return [(pair, LANES, LANES // 2), (pair + 1, LANES, LANES // 2)]


def code_tile(rows_ref, out_ref, first):
    depth = rows_ref.shape[1]
    for low in range(0, depth, LANES):
        out_ref[low : low + LANES, pl.ds(first, 256)] = code_columns(rows_ref[:, low : low + LANES].T)


def fetch_rows(gate_ref, up_ref, tiles, target, arrived):
    experts = gate_ref.shape[0]
    groups = []
    for n, tile in enumerate(tiles):
        group, at = [], 0
        for ref in (gate_ref, up_ref):
            for expert, first, count in tile_rows(tile, experts):
                source = ref.at[expert, first : first + count]
                group.append(pltpu.make_async_copy(source, target.at[n, at : at + count], arrived.at[n, len(group)]))
                at += count
        groups.append(group)
    return groups


def code_kernel(*refs, following):
    if following:
        gate_ref, up_ref, rows_ref, _, out_ref, rest_ref, arrived = refs
        groups = fetch_rows(gate_ref, up_ref, following, rest_ref, arrived)
    else:
        (rows_ref, _, out_ref), groups = refs, []
    for group in groups:
        for copy in group:
            copy.start()

    @pl.loop(0, rows_ref.shape[0])
    def _(n):
        code_tile(rows_ref.at[n], out_ref, pl.multiple_of(n * 256, 256))

    for group in groups:
        for copy in group:
            copy.wait()


def code_weights(gate, up, rows, following, after):
    tiles, _, depth = rows.shape
    outs = [pltpu.VMEM((depth, 256 * tiles), jnp.bfloat16)]
    operands, scratch = [rows, after], []
    spaces = [pltpu.VMEM, pl.ANY]
    if following:
        outs.append(pltpu.VMEM((len(following), 2 * LANES, depth), jnp.bfloat16))
        operands = [pltpu.with_memory_space_constraint(x, pltpu.HBM) for x in (gate, up)] + operands
        spaces = [pl.ANY, pl.ANY] + spaces
        scratch = [pltpu.SemaphoreType.DMA((len(following), 4))]
    return pl.pallas_call(
        functools.partial(code_kernel, following=following),
        out_shape=outs,
        in_specs=[pl.BlockSpec(memory_space=space) for space in spaces],
        out_specs=[pl.BlockSpec(memory_space=pltpu.VMEM)] * len(outs),
        scratch_shapes=scratch,
        compiler_params=pltpu.CompilerParams(vmem_limit_bytes=12 << 20),
        cost_estimate=pl.CostEstimate(flops=1024, bytes_accessed=1024, transcendentals=0),
        name="code",
    )(*operands)


def begin_kernel(
    tokens_ref, ids_ref, weights_ref, gate_ref, up_ref, packed_ref, out_ref, rest_ref, ids, weights, held, near, fetched,
    *, tiles, following,
):
    experts = gate_ref.shape[0]
    rows, width = tokens_ref.shape
    routes = [
        pltpu.make_async_copy(ids_ref, ids, near.at[0]),
        pltpu.make_async_copy(weights_ref, weights, near.at[1]),
    ]
    moved = pltpu.make_async_copy(tokens_ref, packed_ref.at[:, :width], near.at[2])
    now = len(tiles)
    groups = fetch_rows(gate_ref, up_ref, tiles, held, fetched)
    later = fetch_rows(gate_ref, up_ref, following, rest_ref, fetched.at[now:])
    for copy in routes + [moved]:
        copy.start()
    for group in groups + later:
        for copy in group:
            copy.start()
    for copy in routes:
        copy.wait()
    number = lax.broadcasted_iota(jnp.int32, (experts, rows), 0)
    mix = jnp.zeros((experts, rows), jnp.float32)
    for choice in range(ids_ref.shape[0]):
        mix += jnp.where(ids[choice : choice + 1, :] == number, weights[choice : choice + 1, :], 0.0)
    high = mix.astype(jnp.bfloat16).astype(jnp.float32)
    middle = (mix - high).astype(jnp.bfloat16).astype(jnp.float32)
    low = mix - high - middle
    fill = jnp.zeros((LANES - 3 * experts, rows), jnp.float32)
    packed_ref[:, width:] = jnp.concatenate([high, middle, low, fill], axis=0).T.astype(jnp.bfloat16)
    for n, group in enumerate(groups):
        for copy in group:
            copy.wait()
        code_tile(held.at[n], out_ref, 256 * n)
    for group in later:
        for copy in group:
            copy.wait()
    moved.wait()


def begin(tokens, expert_ids, combine_weights, gate, up, tiles, following):
    depth = gate.shape[2]
    rows, width = tokens.shape
    choices = expert_ids.shape[1]
    operands = (tokens, expert_ids.T, combine_weights.T, gate, up)
    return pl.pallas_call(
        functools.partial(begin_kernel, tiles=tiles, following=following),
        out_shape=[
            pltpu.VMEM((rows, width + LANES), jnp.bfloat16),
            pltpu.VMEM((depth, 256 * len(tiles)), jnp.bfloat16),
            pltpu.VMEM((len(following), 2 * LANES, depth), jnp.bfloat16),
        ],
        in_specs=[pl.BlockSpec(memory_space=pl.ANY)] * 5,
        out_specs=[pl.BlockSpec(memory_space=pltpu.VMEM)] * 3,
        scratch_shapes=[
            pltpu.VMEM((choices, rows), jnp.int32),
            pltpu.VMEM((choices, rows), jnp.float32),
            pltpu.VMEM((len(tiles), 2 * LANES, depth), jnp.bfloat16),
            pltpu.SemaphoreType.DMA((3,)),
            pltpu.SemaphoreType.DMA((len(tiles) + len(following), 4)),
        ],
        compiler_params=pltpu.CompilerParams(vmem_limit_bytes=16 << 20),
        cost_estimate=pl.CostEstimate(flops=1024, bytes_accessed=1024, transcendentals=0),
        name="begin",
    )(*(pltpu.with_memory_space_constraint(x, pltpu.HBM) for x in operands))


def hidden_kernel(*refs, count, pieces, after, experts):
    chunks = refs[:count]
    own = refs[count : count + pieces]
    other = refs[count + pieces : count + 2 * pieces]
    *outs, tok = refs[count + 2 * pieces + after :]
    sizes = [chunk.shape[0] for chunk in chunks]
    width = tok.shape[1]
    core = lax.axis_index("tp")
    depth = own[0].shape[0]
    total = tok.shape[0]
    at = 0
    mixes = []
    for chunk, rows in zip(chunks, sizes):
        tok[at : at + rows, :] = chunk[:, :width]
        parts = chunk[:, width : width + LANES].astype(jnp.float32)
        mixes.append(parts[:, :experts] + parts[:, experts : 2 * experts] + parts[:, 2 * experts : 3 * experts])
        at += rows
    if at < total:
        tok[at:, :] = jnp.zeros((total - at, width), tok.dtype)
        mixes.append(jnp.zeros((total - at, experts), jnp.float32))
    mix = jnp.concatenate(mixes, axis=0) if len(mixes) > 1 else mixes[0]
    near = tok[:, pl.ds(pl.multiple_of(core * depth, LANES), depth)]
    far = tok[:, pl.ds(pl.multiple_of((1 - core) * depth, LANES), depth)]
    lane = lax.broadcasted_iota(jnp.int32, (total, LANES), 1)
    first_sum = jnp.zeros((total, LANES), jnp.float32)
    second_sum = jnp.zeros((total, LANES), jnp.float32)
    places = [(piece, at) for piece in range(pieces) for at in range(0, own[piece].shape[1], 256)]
    for tile, (piece, at) in enumerate(places):
        columns = slice(at, at + 256)
        both = jnp.dot(near, own[piece][:, columns], preferred_element_type=jnp.float32)
        both += jnp.dot(far, other[piece][:, columns], preferred_element_type=jnp.float32)
        gate = jnp.minimum(both[:, :LANES], LIMIT)
        up = jnp.clip(both[:, LANES:], -LIMIT, LIMIT)
        active = gate * jax.nn.sigmoid(1.702 * gate) * (up + 1.0)
        active = active.astype(jnp.bfloat16).astype(jnp.float32)
        if tile < experts:
            first_sum += active * mix[:, tile : tile + 1]
        else:
            pair = 2 * (tile - experts)
            second_sum += active * jnp.where(lane < LANES // 2, mix[:, pair : pair + 1], mix[:, pair + 1 : pair + 2])
    last = second_sum[:, : LANES // 2] + second_sum[:, LANES // 2 :]
    at = 0
    for out, rows in zip(outs, sizes):
        out[:, :LANES] = first_sum[at : at + rows].astype(jnp.bfloat16)
        out[:, LANES:] = last[at : at + rows].astype(jnp.bfloat16)
        at += rows


def hidden_units(chunks, own, other, experts, *after):
    units = 3 * LANES // 2
    sizes = [chunk.shape[0] for chunk in chunks]
    total, width = max(sum(sizes), LANES), 2 * own[0].shape[0]
    return pl.pallas_call(
        functools.partial(hidden_kernel, count=len(chunks), pieces=len(own), after=len(after), experts=experts),
        out_shape=[jax.ShapeDtypeStruct((rows, units), jnp.bfloat16) for rows in sizes],
        in_specs=[pl.BlockSpec(memory_space=pltpu.VMEM)] * (len(chunks) + 2 * len(own))
        + [pl.BlockSpec(memory_space=pl.ANY)] * len(after),
        out_specs=[pl.BlockSpec(memory_space=pltpu.VMEM)] * len(chunks),
        scratch_shapes=[pltpu.VMEM((total, width), jnp.bfloat16)],
        compiler_params=pltpu.CompilerParams(vmem_limit_bytes=20 << 20),
        cost_estimate=pl.CostEstimate(flops=12*10**9, bytes_accessed=1024, transcendentals=0),
        name="hidden",
    )(*chunks, *own, *other, *after)


def join_kernel(*refs, steps):
    blocks, out_ref, held = refs[: len(steps)], refs[len(steps)], refs[len(steps) + 1]
    owners = lax.axis_size("ep")
    place = ring_place(lax.axis_index("ep"), owners)
    units = held.shape[2]
    for block, step in zip(blocks, steps):
        source = ring_owner((place + step + owners) % owners, owners)
        width = block.shape[1]
        if width == units:
            held[source] = block[...]
        else:
            held[source, :, :LANES] = block[:, width - LANES :]
            held[source, :, LANES:] = block[:, width - LANES - LANES // 2 : width - LANES]
    for owner in range(owners):
        out_ref[:, owner * units : (owner + 1) * units] = held[owner]


def join_units(blocks, steps, units):
    rows = blocks[0].shape[0]
    return pl.pallas_call(
        functools.partial(join_kernel, steps=steps),
        out_shape=jax.ShapeDtypeStruct((rows, units * len(steps)), jnp.bfloat16),
        in_specs=[pl.BlockSpec(memory_space=pltpu.VMEM)] * len(blocks),
        out_specs=pl.BlockSpec(memory_space=pltpu.VMEM),
        scratch_shapes=[pltpu.VMEM((len(steps), rows, units), jnp.bfloat16)],
        compiler_params=pltpu.CompilerParams(vmem_limit_bytes=4 << 20),
        name="join",
    )(*blocks)


def attach_kernel(chunk_ref, block_ref, out_ref):
    width = chunk_ref.shape[1]
    out_ref[:, : width - LANES] = chunk_ref[:, : width - LANES]
    beside = [chunk_ref[:, width - LANES : width - LANES // 2], block_ref[:, LANES:]]
    out_ref[:, width - LANES : width] = jnp.concatenate(beside, axis=1)
    out_ref[:, width:] = block_ref[:, :LANES]


def attach(chunk, block):
    rows, width = chunk.shape
    return pl.pallas_call(
        attach_kernel,
        out_shape=jax.ShapeDtypeStruct((rows, width + LANES), chunk.dtype),
        in_specs=[pl.BlockSpec(memory_space=pltpu.VMEM)] * 2,
        out_specs=pl.BlockSpec(memory_space=pltpu.VMEM),
        compiler_params=pltpu.CompilerParams(vmem_limit_bytes=4 << 20),
        cost_estimate=pl.CostEstimate(flops=1024, bytes_accessed=1024, transcendentals=0),
        name="attach",
    )(chunk, block)


def mark_kernel(*refs):
    refs[-1][...] = jnp.zeros(refs[-1].shape, refs[-1].dtype)


def mark(*after):
    return pl.pallas_call(
        mark_kernel,
        out_shape=jax.ShapeDtypeStruct((8, LANES), jnp.float32),
        in_specs=[pl.BlockSpec(memory_space=pl.ANY)] * len(after),
        out_specs=pl.BlockSpec(memory_space=pltpu.VMEM),
        compiler_params=pltpu.CompilerParams(vmem_limit_bytes=1 << 20),
        cost_estimate=pl.CostEstimate(flops=6*10**10, bytes_accessed=1024, transcendentals=0),
        name="mark",
    )(*after)


def resident(tokens, expert_ids, combine_weights, gate_weight, up_weight):
    experts = gate_weight.shape[0]
    owners = lax.axis_size("ep")
    tie = lax.optimization_barrier

    def swap(part):
        return lax.ppermute(part, "tp", [(0, 1), (1, 0)])

    def onward(right, left):
        return ring_send(right, owners, 1), ring_send(left, owners, -1)

    tiles = tuple(range(experts * 3 // 2))
    parts = tiles[:1], tiles[1:6], tiles[6:]
    packed, first, rest = begin(tokens, expert_ids, combine_weights, gate_weight, up_weight, *parts[:2])
    right1, left1 = onward(packed, packed)
    own, other = [first], [swap(first)]
    after = other[0]
    for following in parts[2:]:
        coded, rest = code_weights(gate_weight, up_weight, rest, following, after)
        own.append(coded)
        after = coded
    own += code_weights(gate_weight, up_weight, rest, (), after)
    other += [swap(part) for part in own[1:]]

    right1, left1, point = tie((right1, left1, mark(right1, left1, own[-1])))
    right2, left2 = onward(right1, left1)
    from1, back1 = hidden_units([right1, left1], own, other, experts, point)
    right3, left3 = onward(attach(right2, back1), attach(left2, from1))
    done = {-1: right3, 1: left3}
    from2, back2 = hidden_units([right2, left2], own, other, experts)
    done[2], done[-2] = ring_send(from2, owners, -2), ring_send(back2, owners, 2)

    right3, _ = tie((right3, from2))
    left3, _ = tie((left3, back2))
    right4 = ring_send(right3, owners, 1)
    from3, back3 = hidden_units([right3, left3], own, other, experts)
    done[3], done[-3] = ring_send(from3, owners, -3), ring_send(back3, owners, 3)

    right4, _, done[2], done[-2] = tie((right4, from3, done[2], done[-2]))
    (from4,) = hidden_units([right4], own, other, experts)
    done[4] = ring_send(from4, owners, 4)
    (done[0],) = hidden_units([packed], own, other, experts)
    places = tuple(sorted(done))
    return join_units([done[p] for p in places], places, done[0].shape[1])


def block_scale(largest):
    scale = jnp.full(largest.shape, 2.0 ** (-40), jnp.float32)
    for exponent_value in range(-39, 9):
        power = 2.0**exponent_value
        scale = jnp.where(largest >= power, jnp.float32(power), scale)
    return scale * 0.25


def code_blocks(weight):
    shaped = weight.reshape(weight.shape[:-1] + (weight.shape[-1] // 32, 32))
    magnitude = jnp.abs(shaped).astype(jnp.float32)
    scale = block_scale(jnp.max(magnitude, axis=-1))[..., None]
    total = jnp.zeros(magnitude.shape, jnp.float32)
    for bound_value, step_value in zip(THRESHOLDS, STEPS_UP):
        total = total + jnp.where(magnitude > bound_value * scale, step_value, 0.0)
    signed = jnp.where(shaped < 0, -total, total) * scale
    return signed.reshape(weight.shape).astype(jnp.bfloat16)


def activate(gate_value, up_value):
    gate_clamped = jnp.minimum(gate_value, LIMIT)
    up_clamped = jnp.clip(up_value, -LIMIT, LIMIT)
    return gate_clamped * jax.nn.sigmoid(1.702 * gate_clamped) * (up_clamped + 1.0)


def dispatched(tokens, expert_ids, combine_weights, gate_weight, up_weight):
    experts = gate_weight.shape[0]
    owners = lax.axis_size("ep")
    cores = lax.axis_size("tp")
    tok_rows = tokens.shape[0]
    top_count = expert_ids.shape[1]
    width = tokens.shape[1]
    slots = max(2, 2 * tok_rows * top_count // experts)
    gate_split, up_split = (
        lax.all_to_all(gate_weight, "tp", split_axis=1, concat_axis=2, tiled=True),
        lax.all_to_all(up_weight, "tp", split_axis=1, concat_axis=2, tiled=True),
    )
    gate_local, up_local = (
        lax.all_to_all(gate_split, "ep", split_axis=0, concat_axis=1, tiled=True),
        lax.all_to_all(up_split, "ep", split_axis=0, concat_axis=1, tiled=True),
    )
    gate_coded = code_blocks(gate_local[0])
    up_coded = code_blocks(up_local[0])
    chosen = expert_ids.reshape(-1)
    onehot = (chosen[:, None] == jnp.arange(experts, dtype=jnp.int32)[None, :]).astype(jnp.int32)
    before = jnp.cumsum(onehot, axis=0, dtype=jnp.int32) - onehot
    ranking = jnp.sum(before * onehot, axis=1, dtype=jnp.int32)
    target = chosen * slots + ranking
    repeated = jnp.repeat(tokens, top_count, axis=0)
    outgoing = jnp.zeros((experts * slots, width), jnp.bfloat16).at[target].set(repeated)
    received = lax.all_to_all(
        outgoing.reshape(experts, slots, width), "ep", split_axis=0, concat_axis=0, tiled=True
    )
    piece = lax.all_gather(received.reshape(owners * slots, width), "tp", axis=0, tiled=True)
    gate_value = jnp.einsum("rd,fd->rf", piece, gate_coded, preferred_element_type=jnp.float32)
    up_value = jnp.einsum("rd,fd->rf", piece, up_coded, preferred_element_type=jnp.float32)
    actives = activate(gate_value, up_value).astype(jnp.bfloat16)
    shaped_back = actives.reshape(cores, owners, slots, actives.shape[1])
    returned = lax.all_to_all(
        lax.all_to_all(shaped_back, "ep", split_axis=1, concat_axis=1, tiled=True),
        "tp",
        split_axis=0,
        concat_axis=3,
        tiled=True,
    )
    flat_back = returned.reshape(experts * slots, returned.shape[3])
    values = flat_back[target].reshape(tok_rows, top_count, flat_back.shape[1])
    mixed = jnp.einsum("tk,tkf->tf", combine_weights, values.astype(jnp.float32))
    hidden_total = mixed.shape[1]
    quarter = hidden_total // (owners * cores)
    mixed = (
        mixed.reshape(tok_rows, cores, owners, quarter)
        .transpose(0, 2, 1, 3)
        .reshape(tok_rows, hidden_total)
    )
    return mixed.astype(jnp.bfloat16)


def per_device(tokens, expert_ids, combine_weights, gate_weight, up_weight):
    experts, units, depth = gate_weight.shape
    owners, cores = lax.axis_size("ep"), lax.axis_size("tp")
    fits = owners == 8 and cores == 2 and experts <= 4 * expert_ids.shape[1] and experts % 8 == 0
    fits = fits and units == 3 * LANES // 2 and depth % 256 == 0 and tokens.shape[0] % 64 == 0
    plan = resident if fits else dispatched
    return plan(tokens, expert_ids, combine_weights, gate_weight, up_weight)


def solution(mesh):
    return jax.shard_map(
        per_device,
        mesh=mesh,
        in_specs=(
            P(("groups", "ep", "tp"), None),
            P(("groups", "ep", "tp"), None),
            P(("groups", "ep", "tp"), None),
            P(None, "ep", "tp"),
            P(None, "ep", "tp"),
        ),
        out_specs=P(("groups", "ep", "tp"), None),
        check_vma=False,
    )
```
